256 devices in a mesh: seq: 32 (over y, x, core), head: 8 (over z).
Axes of the slice: x: 4, y: 4, z: 8, core: 2. Of those that a mesh axis runs over, the one named last changes fastest.
Arguments:
- q_values: bfloat16 [65536, 4096], P('seq', 'head'), may hold values from -6 to 6
- k_values: bfloat16 [65536, 4096], P('seq', 'head'), may hold values from -6 to 6
- v_values: bfloat16 [65536, 4096], P('seq', 'head'), may hold values from -6 to 6
- q_scales: float32 [65536, 32], P('seq', 'head'), may hold values from 0.5 to 4
- k_scales: float32 [65536, 32], P('seq', 'head'), may hold values from 0.5 to 4
- v_scales: float32 [65536, 32], P('seq', 'head'), may hold values from 0.5 to 2
- conv_weight: float32 [32, 33], P('head'), may hold values from -0.9 to 0.9
Outputs:
- attended: bfloat16 [65536, 4096], P('seq', 'head')
The draws below stay inside these ranges and needn't reach their ends.
All inputs are finite; a program needn't handle non-finite values.
Results may differ from the reference program's by a relative error of at most 0.03.
Values may be sent and summed in bfloat16 or wider, within the bound.
A program may use at most 128 MiB of HBM per device.

```python
import math
import jax
import jax.numpy as jnp
from jax import lax

HEADS = 32
HEAD_DIM = 128
LANDMARKS = 256
CONV = 33
SWEEPS = 6
SEQ = 65536


def shaped_field(key, which):
    segment = SEQ // LANDMARKS
    own_key = jax.random.fold_in(key, which)
    noise_key, direction_key, spread_key = jax.random.split(own_key, 3)
    noise = jax.random.normal(noise_key, (LANDMARKS, segment, HEADS, HEAD_DIM), jnp.float32)
    direction = jax.random.normal(direction_key, (LANDMARKS, 1, HEADS, HEAD_DIM), jnp.float32)
    spread = jnp.exp(jax.random.uniform(spread_key, (LANDMARKS, 1, HEADS, 1), jnp.float32, math.log(0.3), math.log(1.2)))
    offset = direction * spread
    field = jnp.clip(noise + offset, -6.0, 6.0)
    return field.reshape(SEQ, HEADS * HEAD_DIM).astype(jnp.bfloat16)


def draw_q_values(key, part):
    return shaped_field(key, 1)


def draw_k_values(key, part):
    return shaped_field(key, 2)


def block_levels(key, extent, pieces, smallest, top_value):
    def one(position, shards_of):
        steps = jax.random.uniform(jax.random.fold_in(jax.random.fold_in(key, 6), position), (shards_of,), jnp.float32, smallest / len(pieces), top_value / len(pieces))
        return jnp.repeat(jnp.exp(steps), extent[position] // shards_of).reshape((-1,) + (1,) * (len(extent) - position - 1))

    gain = one(*pieces[0])
    for cut in pieces[1:]:
        gain = gain * one(*cut)
    return gain


def centred(rng, dims, scale, limit, pieces=(), kind=jnp.bfloat16):
    factor_of = block_levels(rng, dims, pieces, -0.22, 0.18) if pieces else 1.0
    values = jax.random.normal(rng, dims, jnp.float32) * scale * factor_of
    return jnp.minimum(jnp.maximum(values, -limit), limit).astype(kind)


def setup_inputs(seed: int = 0) -> dict:
    seeds = jax.random.split(jax.random.key(seed), 8)
    return {
        "q_values": draw_q_values(jax.random.fold_in(seeds[7], 71), 0),
        "k_values": draw_k_values(jax.random.fold_in(seeds[7], 71), 0),
        "v_values": centred(seeds[2], (SEQ, HEADS * HEAD_DIM), 1.0, 6.0, ((0, 32), (1, 8))),
        "q_scales": jnp.clip(jnp.exp(math.log(4.0) - 2.0794415 * jax.random.uniform(seeds[3], (SEQ, HEADS), jnp.float32) ** block_levels(seeds[3], (SEQ, HEADS), ((0, 32), (1, 8)), -0.2, 0.2)), 0.5, 4.0),
        "k_scales": jnp.clip(jnp.exp(math.log(4.0) - 2.0794415 * jax.random.uniform(seeds[4], (SEQ, HEADS), jnp.float32) ** block_levels(seeds[4], (SEQ, HEADS), ((0, 32), (1, 8)), -0.2, 0.2)), 0.5, 4.0),
        "v_scales": jnp.clip(jnp.exp(math.log(2.0) - 1.3862944 * jax.random.uniform(seeds[5], (SEQ, HEADS), jnp.float32) ** block_levels(seeds[5], (SEQ, HEADS), ((0, 32), (1, 8)), -0.2, 0.2)), 0.5, 2.0),
        "conv_weight": centred(seeds[6], (HEADS, CONV), 0.15, 0.9, ((0, 8),), jnp.float32),
    }


def dequant(value_rows, scales):
    count = scales.shape[1]
    shaped = value_rows.reshape(value_rows.shape[0], count, HEAD_DIM).astype(jnp.float32)
    return (shaped * scales[:, :, None]).astype(jnp.bfloat16)


def newton(kernel, initial, right_side):
    highest = lax.Precision.HIGHEST
    eye_matrix = jnp.eye(kernel.shape[0], dtype=jnp.float32)
    iterate = initial
    for sweep in range(SWEEPS):
        product = jnp.dot(kernel, iterate, precision=highest)
        inner_term = 7.0 * eye_matrix - product
        inner_term = 15.0 * eye_matrix - jnp.dot(product, inner_term, precision=highest)
        inner_term = 13.0 * eye_matrix - jnp.dot(product, inner_term, precision=highest)
        iterate = 0.25 * jnp.dot(iterate, inner_term, precision=highest)
    return jnp.dot(iterate, right_side, precision=highest).astype(jnp.bfloat16)


def reference(q_values, k_values, v_values, q_scales, k_scales, v_scales, conv_weight):
    total_rows = q_values.shape[0]
    query_rows = dequant(q_values, q_scales)
    key_rows = dequant(k_values, k_scales)
    value_rows = dequant(v_values, v_scales)
    segment = total_rows // LANDMARKS

    def means(source):
        shaped = source.reshape(LANDMARKS, segment, HEADS, HEAD_DIM).astype(jnp.float32)
        return jnp.mean(shaped, axis=1).astype(jnp.bfloat16)

    query_landmarks = means(query_rows)
    key_landmarks = means(key_rows)
    pseudo_inverse_factor = HEAD_DIM ** -0.5
    landmark_kernel = jnp.einsum("jvc,kvc->vjk", query_landmarks.astype(jnp.float32), key_landmarks.astype(jnp.float32)) * pseudo_inverse_factor
    middle = jax.nn.softmax(landmark_kernel, axis=-1)
    col_top = jnp.max(jnp.sum(middle, axis=1))
    row_top = jnp.max(jnp.sum(middle, axis=2))
    start = jnp.swapaxes(middle, 1, 2) / (col_top * row_top)
    reach = CONV // 2

    def per_head(operands):
        query_head, key_head, value_head, middle_head, start_head, qmark_head, kmark_head, taps = operands
        distant_term = jnp.dot(qmark_head, key_head.T, preferred_element_type=jnp.float32) * pseudo_inverse_factor
        weight_matrix = jnp.exp(distant_term - jnp.max(distant_term, axis=1, keepdims=True))
        total = jnp.sum(weight_matrix, axis=1)
        summed = jnp.dot(weight_matrix.astype(jnp.bfloat16), value_head, preferred_element_type=jnp.float32)
        reduced = summed / total[:, None]
        projected_values = newton(middle_head, start_head, reduced)
        near_scores = jnp.dot(query_head, kmark_head.T, preferred_element_type=jnp.float32) * pseudo_inverse_factor
        local_term = jax.nn.softmax(near_scores, axis=-1).astype(jnp.bfloat16)
        attended = jnp.dot(local_term, projected_values, preferred_element_type=jnp.float32)
        padded = jnp.pad(value_head, ((reach, reach), (0, 0)))
        mixed = jnp.zeros((total_rows, HEAD_DIM), jnp.float32)
        for tap_index in range(CONV):
            mixed = mixed + padded[tap_index:tap_index + total_rows].astype(jnp.float32) * taps[tap_index]
        return (attended + mixed).astype(jnp.bfloat16)

    stacked = lax.map(per_head, (jnp.swapaxes(query_rows, 0, 1), jnp.swapaxes(key_rows, 0, 1), jnp.swapaxes(value_rows, 0, 1), middle, start, jnp.swapaxes(query_landmarks, 0, 1), jnp.swapaxes(key_landmarks, 0, 1), conv_weight))
    return jnp.swapaxes(stacked, 0, 1).reshape(total_rows, HEADS * HEAD_DIM)
```

```python
import functools
import math

import jax
import jax.numpy as jnp
from jax import lax
from jax.experimental import pallas as pl
from jax.experimental.pallas import tpu as pltpu
from jax.sharding import PartitionSpec as P

MESH = pl.DeviceIdType.MESH
F32 = jnp.float32
BF16 = jnp.bfloat16
HEAD_DIM = 128
LANDMARKS = 256
SWEEPS = 6
TAPS = 33
REACH = TAPS // 2
LOG2E = math.log2(math.e)
SCALE2 = HEAD_DIM**-0.5 * LOG2E
FACTOR = HEAD_DIM**-0.5

TOK = 2048
HEADS = 4
WIDTH = HEADS * HEAD_DIM
SEQN = 32
HEADN = 8
SEGS = 8
SEG = 256
OWN = 8
SLICE = HEAD_DIM // OWN
PACK = LANDMARKS + 128
NEAR_EARLY = 2


def dot(a, b):
    return jnp.dot(a, b, preferred_element_type=F32)


def dot_nt(a, b):
    return lax.dot_general(a, b, (((1,), (1,)), ((), ())), preferred_element_type=F32)


def cols(h):
    return slice(h * HEAD_DIM, (h + 1) * HEAD_DIM)


def kernel(
    q_hbm, k_hbm, v_hbm, qs_ref, ks_ref, vs_ref, cw_ref, out_hbm,
    q_v, k_v, v_raw, v_pad, vt, sc_qk, sc_v, lm_all, qm, km,
    mid, tops, score, wt, rs_send, rs_recv, x_ref, near, conv, mp_all, out_v, wpad, toep,
    q_sem, k_sem, v_sem, out_sem, lm_s, lm_r, halo_s, halo_r, top_s, top_r, rs_s, rs_r, mp_s, mp_r,
):
    me = lax.axis_index("seq")
    zme = lax.axis_index("head")
    yme, xme, cme = me // 8, (me // 2) % 4, me % 2
    h_me = 2 * ((xme + yme) % 2) + cme
    j_me = (me // 2) // 2
    b_me = h_me * OWN + j_me

    def partner(r):
        return (
            ((yme + r // 8) % 4) * 8 + ((xme + (r // 2) % 4) % 4) * 2 + (cme + r % 2) % 2
        )

    def owner(h, j):
        y = j // 2
        return (4 * y + 2 * (j % 2) + (h // 2 + y) % 2) * 2 + h % 2

    def rows_copy(src, dst, sem, i):
        rows = pl.ds(i * SEG, SEG)
        return pltpu.make_async_copy(src.at[rows], dst.at[rows], sem.at[i])

    for i in range(SEGS):
        rows_copy(q_hbm, q_v, q_sem, i).start()
        rows_copy(k_hbm, k_v, k_sem, i).start()
    for i in range(SEGS):
        rows_copy(v_hbm, v_raw, v_sem, i).start()

    barrier = pltpu.get_barrier_semaphore()

    def greet_seq(r, _):
        pl.semaphore_signal(barrier, inc=1, device_id=(partner(r), zme), device_id_type=MESH)
        return 0

    def greet_head(r, _):
        pl.semaphore_signal(
            barrier, inc=1, device_id=(me, (zme + r) % HEADN), device_id_type=MESH
        )
        return 0

    lax.fori_loop(1, SEQN, greet_seq, 0)
    lax.fori_loop(1, HEADN, greet_head, 0)

    sc_qk[...] = jnp.concatenate([qs_ref[...], ks_ref[...]], axis=0).T
    sc_v[...] = jnp.concatenate([vs_ref[...], vs_ref[...]], axis=0).T

    seg_id = lax.broadcasted_iota(jnp.int32, (SEGS, HEAD_DIM), 0)

    def scale_qk(i, marks):
        rows = pl.ds(pl.multiple_of(i * SEG, SEG), SEG)
        rows_copy(q_hbm, q_v, q_sem, i).wait()
        rows_copy(k_hbm, k_v, k_sem, i).wait()
        following = []
        for n in range(2 * HEADS):
            buf, h = (q_v, n) if n < HEADS else (k_v, n - HEADS)
            x = (buf[rows, cols(h)].astype(F32) * sc_qk[rows, n : n + 1]).astype(BF16)
            buf[rows, cols(h)] = x
            mean = jnp.sum(x.astype(F32), axis=0, keepdims=True) * (1.0 / SEG)
            following.append(jnp.where(seg_id == i, mean, marks[n]))
        return tuple(following)

    marks = lax.fori_loop(
        0, SEGS, scale_qk, (jnp.zeros((SEGS, HEAD_DIM), F32),) * (2 * HEADS)
    )
    for h in range(HEADS):
        both = jnp.concatenate([marks[h], marks[HEADS + h]], axis=0)
        lm_all[me, :, cols(h)] = both.astype(BF16)

    pl.semaphore_wait(barrier, SEQN - 1 + HEADN - 1)

    def lm_copy(r, slot):
        return pltpu.make_async_remote_copy(
            src_ref=lm_all.at[slot],
            dst_ref=lm_all.at[slot],
            send_sem=lm_s.at[r],
            recv_sem=lm_r.at[slot],
            device_id=(partner(r), zme),
            device_id_type=MESH,
        )

    def send_lm(r, _):
        lm_copy(r, me).start()
        return 0

    lax.fori_loop(1, SEQN, send_lm, 0)

    def scale_v(i, _):
        rows = pl.ds(pl.multiple_of(i * SEG, SEG), SEG)
        out_rows = pl.ds(pl.multiple_of(i * SEG + REACH, REACH), SEG)
        rows_copy(v_hbm, v_raw, v_sem, i).wait()
        for h in range(HEADS):
            x = (v_raw[rows, cols(h)].astype(F32) * sc_v[rows, h : h + 1]).astype(BF16)
            v_pad[out_rows, cols(h)] = x
            vt[h, :, rows] = x.astype(F32).T.astype(BF16)
        return 0

    lax.fori_loop(0, SEGS, scale_v, 0)
    v_pad[TOK + 2 * REACH :, :] = jnp.zeros((128 - 2 * REACH, WIDTH), BF16)

    after, before = (me + 1) % SEQN, (me + SEQN - 1) % SEQN
    down = pltpu.make_async_remote_copy(
        src_ref=v_pad.at[pl.ds(TOK, REACH)],
        dst_ref=v_pad.at[pl.ds(0, REACH)],
        send_sem=halo_s.at[0],
        recv_sem=halo_r.at[0],
        device_id=(after, zme),
        device_id_type=MESH,
    )
    up = pltpu.make_async_remote_copy(
        src_ref=v_pad.at[pl.ds(REACH, REACH)],
        dst_ref=v_pad.at[pl.ds(TOK + REACH, REACH)],
        send_sem=halo_s.at[1],
        recv_sem=halo_r.at[1],
        device_id=(before, zme),
        device_id_type=MESH,
    )
    down.start()
    up.start()

    wpad[...] = jnp.zeros_like(wpad)
    wpad[0:HEADS, 0:TAPS] = cw_ref[...]
    for h in range(HEADS):
        line = jnp.broadcast_to(wpad[h : h + 1, :], (128, 256))
        toep[h] = pltpu.roll(line, 0, 1, stride=1, stride_axis=0).astype(BF16)

    def conv_block(b):
        window = pl.ds(pl.multiple_of(b * 128, 128), 256)
        rows = pl.ds(pl.multiple_of(b * 128, 128), 128)
        for h in range(HEADS):
            conv[rows, cols(h)] = dot(toep[h], v_pad[window, cols(h)])

    def conv_inner(b, _):
        conv_block(b)
        return 0

    lax.fori_loop(1, TOK // 128 - 1, conv_inner, 0)

    def recv_lm(r, _):
        lm_copy(r, partner(r)).wait_recv()
        return 0

    lax.fori_loop(1, SEQN, recv_lm, 0)
    for h in range(HEADS):
        both = lm_all[:, :, cols(h)].astype(F32)
        qm[h] = both[:, :SEGS].reshape(LANDMARKS, HEAD_DIM).astype(BF16)
        km[h] = both[:, SEGS:].reshape(LANDMARKS, HEAD_DIM).astype(BF16)

    col_top = jnp.zeros((1, 1), F32)
    row_top = jnp.zeros((1, 1), F32)
    for h in range(HEADS):
        s = dot_nt(qm[h], km[h])
        e = jnp.exp2((s - jnp.max(s, axis=1, keepdims=True)) * SCALE2)
        m = e / jnp.sum(e, axis=1, keepdims=True)
        mid[h] = m
        c = jnp.sum(m, axis=0, keepdims=True)
        r = jnp.sum(m, axis=1, keepdims=True)
        col_top = jnp.maximum(col_top, jnp.max(c, axis=1, keepdims=True))
        row_top = jnp.maximum(row_top, jnp.max(r, axis=0, keepdims=True))
    first_half = lax.broadcasted_iota(jnp.int32, (8, 128), 0) < 4
    tops[zme] = jnp.where(
        first_half, jnp.broadcast_to(col_top, (8, 128)), jnp.broadcast_to(row_top, (8, 128))
    )

    def top_copy(r, slot):
        return pltpu.make_async_remote_copy(
            src_ref=tops.at[slot],
            dst_ref=tops.at[slot],
            send_sem=top_s.at[r],
            recv_sem=top_r.at[slot],
            device_id=(me, (zme + r) % HEADN),
            device_id_type=MESH,
        )

    def send_top(r, _):
        top_copy(r, zme).start()
        return 0

    lax.fori_loop(1, HEADN, send_top, 0)

    def rs_copy(block, slot, target):
        return pltpu.make_async_remote_copy(
            src_ref=rs_send.at[block],
            dst_ref=rs_recv.at[slot],
            send_sem=rs_s.at[block],
            recv_sem=rs_r.at[slot],
            device_id=(target, zme),
            device_id_type=MESH,
        )

    row_id = lax.broadcasted_iota(jnp.int32, (SLICE, 128), 0)
    for h in range(HEADS):
        def far_scores(i, top):
            rows = pl.ds(pl.multiple_of(i * SEG, SEG), SEG)
            s = dot_nt(k_v[rows, cols(h)], qm[h])
            score[rows, :] = s
            return jnp.maximum(top, jnp.max(s.reshape(SEG // 8, 8, LANDMARKS), axis=0))

        top = lax.fori_loop(0, SEGS, far_scores, jnp.full((8, LANDMARKS), -jnp.inf, F32))
        top = jnp.max(top, axis=0, keepdims=True).astype(BF16).astype(F32)

        def far_weights(i, total):
            rows = pl.ds(pl.multiple_of(i * SEG, SEG), SEG)
            e = jnp.exp2((score[rows, :] - top) * SCALE2)
            wt[rows, :] = e.astype(BF16)
            return total + jnp.sum(e.reshape(SEG // 8, 8, LANDMARKS), axis=0)

        total = lax.fori_loop(0, SEGS, far_weights, jnp.zeros((8, LANDMARKS), F32))
        total = jnp.sum(total, axis=0, keepdims=True)
        total_hi = total.astype(BF16).astype(F32)
        total_lo = total - total_hi
        summed = dot(vt[h], wt[...])
        facts = jnp.zeros((SLICE, 128), F32)
        for n, (vec, half) in enumerate(
            (v, half) for v in (top, total_hi, total_lo) for half in range(2)
        ):
            part = jnp.broadcast_to(vec[:, half * 128 : (half + 1) * 128], (SLICE, 128))
            facts = jnp.where(row_id == n, part, facts)
        rs_send[h * OWN : (h + 1) * OWN, :, 0:LANDMARKS] = (
            summed.astype(BF16).reshape(OWN, SLICE, LANDMARKS)
        )
        rs_send[h * OWN : (h + 1) * OWN, :, LANDMARKS:PACK] = jnp.broadcast_to(
            facts.astype(BF16)[None], (OWN, SLICE, 128)
        )

        def send_rs(n, _):
            j = (n + j_me) % OWN
            target = owner(h, j)
            block = h * OWN + j

            @pl.when(target != me)
            def _():
                rs_copy(block, me, target).start()

            return 0

        lax.fori_loop(0, OWN, send_rs, 0)
    rs_recv[me] = rs_send[b_me]

    down.wait_recv()
    up.wait_recv()
    v_pad[0:REACH, :] = jnp.where(me == 0, jnp.zeros((REACH, WIDTH), BF16), v_pad[0:REACH, :])
    v_pad[TOK + REACH : TOK + 2 * REACH, :] = jnp.where(
        me == SEQN - 1, jnp.zeros((REACH, WIDTH), BF16), v_pad[TOK + REACH : TOK + 2 * REACH, :]
    )
    conv_block(0)
    conv_block(TOK // 128 - 1)

    def recv_top(r, _):
        top_copy(r, (zme + r) % HEADN).wait_recv()
        return 0

    lax.fori_loop(1, HEADN, recv_top, 0)
    best = jnp.max(tops[...], axis=0)
    scale = 1.0 / (best[0:1, 0:1] * best[4:5, 0:1])
    m = mid[h_me]
    mb = m.astype(BF16)
    x_ref[0:LANDMARKS, :] = dot(m.T.astype(BF16), mb) * scale
    x_ref[LANDMARKS:, :] = m * scale

    def sweep(_, carry):
        x = x_ref[...]
        xb = x.astype(BF16)
        y = dot(xb, xb[:LANDMARKS])
        b = (7.0 * x[:LANDMARKS] - y[:LANDMARKS]).astype(BF16)
        x_ref[...] = 0.25 * (13.0 * x - 15.0 * y + dot(y.astype(BF16), b))
        return carry

    lax.fori_loop(0, SWEEPS, sweep, 0)

    def near_softmax(h):
        def chunk(i, _):
            rows = pl.ds(pl.multiple_of(i * 128, 128), 128)
            s = dot_nt(q_v[rows, cols(h)], km[h])
            e = jnp.exp2((s - jnp.max(s, axis=1, keepdims=True)) * SCALE2)
            near[h, rows, :] = (e * (1.0 / jnp.sum(e, axis=1, keepdims=True))).astype(BF16)
            return 0

        lax.fori_loop(0, TOK // 128, chunk, 0)

    for h in range(NEAR_EARLY):
        near_softmax(h)

    def recv_rs(r, _):
        rs_copy(0, partner(r), me).wait_recv()
        return 0

    lax.fori_loop(1, SEQN, recv_rs, 0)

    def facts_top(s, top):
        return jnp.maximum(top, rs_recv[s, :, LANDMARKS:PACK].astype(F32))

    top = lax.fori_loop(0, SEQN, facts_top, jnp.full((SLICE, 128), -jnp.inf, F32))

    def combine(s, carry):
        num, den = carry
        facts = rs_recv[s, :, LANDMARKS:PACK].astype(F32)
        e = jnp.exp2((facts - top) * SCALE2)
        w = jnp.concatenate([e[0:1], e[1:2]], axis=1)
        part = jnp.concatenate([facts[2:3] + facts[4:5], facts[3:4] + facts[5:6]], axis=1)
        return num + rs_recv[s, :, 0:LANDMARKS].astype(F32) * w, den + part * w

    num, den = lax.fori_loop(
        0, SEQN, combine, (jnp.zeros((SLICE, LANDMARKS), F32), jnp.zeros((1, LANDMARKS), F32))
    )
    reduced = (num / den).astype(BF16)
    mp_all[b_me] = dot(reduced, x_ref[LANDMARKS:, :].astype(BF16)).astype(BF16)

    def mp_copy(r, slot):
        return pltpu.make_async_remote_copy(
            src_ref=mp_all.at[slot],
            dst_ref=mp_all.at[slot],
            send_sem=mp_s.at[r],
            recv_sem=mp_r.at[slot],
            device_id=(partner(r), zme),
            device_id_type=MESH,
        )

    def send_mp(r, _):
        mp_copy(r, b_me).start()
        return 0

    lax.fori_loop(1, SEQN, send_mp, 0)

    for h in range(NEAR_EARLY, HEADS):
        near_softmax(h)

    for h in range(HEADS):
        for j in range(OWN):
            b = h * OWN + j

            @pl.when(b != b_me)
            def _():
                mp_copy(0, b).wait_recv()

    mapped = [
        mp_all[h * OWN : (h + 1) * OWN].reshape(HEAD_DIM, LANDMARKS).astype(F32).T.astype(BF16)
        for h in range(HEADS)
    ]
    step = 512
    for i in range(TOK // step):
        rows = slice(i * step, (i + 1) * step)
        for h in range(HEADS):
            out_v[rows, cols(h)] = (dot(near[h, rows, :], mapped[h]) + conv[rows, cols(h)]).astype(
                BF16
            )
        pltpu.make_async_copy(out_v.at[rows], out_hbm.at[rows], out_sem.at[i]).start()

    down.wait_send()
    up.wait_send()

    def sent(r, _):
        lm_copy(r, me).wait_send()
        mp_copy(r, b_me).wait_send()
        return 0

    lax.fori_loop(1, SEQN, sent, 0)

    def sent_top(r, _):
        top_copy(r, zme).wait_send()
        return 0

    lax.fori_loop(1, HEADN, sent_top, 0)

    def sent_rs(b, _):
        @pl.when(b != b_me)
        def _():
            rs_copy(b, me, me).wait_send()

        return 0

    lax.fori_loop(0, SEQN, sent_rs, 0)
    for i in range(TOK // step):
        rows = slice(i * step, (i + 1) * step)
        pltpu.make_async_copy(out_v.at[rows], out_hbm.at[rows], out_sem.at[i]).wait()


def shards(q, k, v, qs, ks, vs, cw):
    dma = pltpu.SemaphoreType.DMA
    vm = pltpu.VMEM
    whole = pl.BlockSpec(memory_space=pltpu.VMEM)
    hbm = pl.BlockSpec(memory_space=pl.ANY)
    return pl.pallas_call(
        kernel,
        out_shape=jax.ShapeDtypeStruct((TOK, WIDTH), BF16),
        in_specs=[hbm, hbm, hbm, whole, whole, whole, whole],
        out_specs=hbm,
        scratch_shapes=[
            vm((TOK, WIDTH), BF16),
            vm((TOK, WIDTH), BF16),
            vm((TOK, WIDTH), BF16),
            vm((TOK + 128, WIDTH), BF16),
            vm((HEADS, HEAD_DIM, TOK), BF16),
            vm((TOK, 8), F32),
            vm((TOK, 8), F32),
            vm((SEQN, 2 * SEGS, WIDTH), BF16),
            vm((HEADS, LANDMARKS, HEAD_DIM), BF16),
            vm((HEADS, LANDMARKS, HEAD_DIM), BF16),
            vm((HEADS, LANDMARKS, LANDMARKS), F32),
            vm((HEADN, 8, 128), F32),
            vm((TOK, LANDMARKS), F32),
            vm((TOK, LANDMARKS), BF16),
            vm((SEQN, SLICE, PACK), BF16),
            vm((SEQN, SLICE, PACK), BF16),
            vm((2 * LANDMARKS, LANDMARKS), F32),
            vm((HEADS, TOK, LANDMARKS), BF16),
            vm((TOK, WIDTH), F32),
            vm((SEQN, SLICE, LANDMARKS), BF16),
            vm((TOK, WIDTH), BF16),
            vm((8, 256), F32),
            vm((HEADS, 128, 256), BF16),
            dma((SEGS,)),
            dma((SEGS,)),
            dma((SEGS,)),
            dma((4,)),
            dma((SEQN,)),
            dma((SEQN,)),
            dma((2,)),
            dma((2,)),
            dma((HEADN,)),
            dma((HEADN,)),
            dma((SEQN,)),
            dma((SEQN,)),
            dma((SEQN,)),
            dma((SEQN,)),
        ],
        compiler_params=pltpu.CompilerParams(
            collective_id=0, has_side_effects=True, vmem_limit_bytes=48 * 1024 * 1024
        ),
        name="nystrom",
    )(q, k, v, qs.T, ks.T, vs.T, cw)


def solution(mesh):
    tokens, heads = P("seq", "head"), P("head", None)
    return jax.shard_map(
        shards, mesh=mesh, in_specs=(tokens,) * 6 + (heads,), out_specs=tokens, check_vma=False
    )
```

```python
import functools
import math

import jax
import jax.numpy as jnp
from jax import lax
from jax.experimental import pallas as pl
from jax.experimental.pallas import tpu as pltpu
from jax.sharding import PartitionSpec as P

MESH = pl.DeviceIdType.MESH
F32 = jnp.float32
BF16 = jnp.bfloat16
HEAD_DIM = 128
LANDMARKS = 256
SWEEPS = 6
TAPS = 33
REACH = TAPS // 2
LOG2E = math.log2(math.e)
SCALE2 = HEAD_DIM**-0.5 * LOG2E
FACTOR = HEAD_DIM**-0.5

TOK = 2048
HEADS = 4
WIDTH = HEADS * HEAD_DIM
SEQN = 32
HEADN = 8
SEGS = 8
SEG = 256
OWN = 8
SLICE = HEAD_DIM // OWN
PACK = LANDMARKS + 128
NEAR_EARLY = 4


def dot(a, b):
    return jnp.dot(a, b, preferred_element_type=F32)


def dot_nt(a, b):
    return lax.dot_general(a, b, (((1,), (1,)), ((), ())), preferred_element_type=F32)


def cols(h):
    return slice(h * HEAD_DIM, (h + 1) * HEAD_DIM)


def kernel(
    q_hbm, k_hbm, v_hbm, qs_hbm, ks_hbm, vs_hbm, cw_hbm, out_hbm,
    scales, taps, q_v, k_v, v_raw, v_pad, vt, sc_qk, sc_v, lm_all, qm, km, kmt,
    mid, tops, score, wt, rs_send, rs_recv, x_ref, near, conv, mp_all, out_v, wpad, toep,
    sc_sem, q_sem, k_sem, v_sem, out_sem, lm_s, lm_r, halo_s, halo_r, top_s, top_r, rs_s, rs_r, mp_s, mp_r,
):
    me = lax.axis_index("seq")
    zme = lax.axis_index("head")
    yme, xme, cme = me // 8, (me // 2) % 4, me % 2
    h_me = 2 * ((xme + yme) % 2) + cme
    j_me = (me // 2) // 2
    b_me = h_me * OWN + j_me

    def partner(r):
        return (
            ((yme + r // 8) % 4) * 8 + ((xme + (r // 2) % 4) % 4) * 2 + (cme + r % 2) % 2
        )

    def owner(h, j):
        y = j // 2
        return (4 * y + 2 * (j % 2) + (h // 2 + y) % 2) * 2 + h % 2

    def rows_copy(src, dst, sem, i):
        rows = pl.ds(i * SEG, SEG)
        return pltpu.make_async_copy(src.at[rows], dst.at[rows], sem.at[i])

    small = [
        pltpu.make_async_copy(src, dst, sc_sem.at[n])
        for n, (src, dst) in enumerate(
            (
                (qs_hbm, scales.at[0]),
                (ks_hbm, scales.at[1]),
                (vs_hbm, scales.at[2]),
                (cw_hbm, taps),
            )
        )
    ]
    for copy in small:
        copy.start()
    for i in range(SEGS):
        rows_copy(q_hbm, q_v, q_sem, i).start()
        rows_copy(k_hbm, k_v, k_sem, i).start()
    for i in range(SEGS):
        rows_copy(v_hbm, v_raw, v_sem, i).start()

    barrier = pltpu.get_barrier_semaphore()

    def greet_seq(r, _):
        pl.semaphore_signal(barrier, inc=1, device_id=(partner(r), zme), device_id_type=MESH)
        return 0

    def greet_head(r, _):
        pl.semaphore_signal(
            barrier, inc=1, device_id=(me, (zme + r) % HEADN), device_id_type=MESH
        )
        return 0

    lax.fori_loop(1, SEQN, greet_seq, 0)
    lax.fori_loop(1, HEADN, greet_head, 0)

    for copy in small:
        copy.wait()
    sc_qk[...] = jnp.concatenate([scales[0], scales[1]], axis=0).T
    sc_v[...] = jnp.concatenate([scales[2], scales[2]], axis=0).T

    seg_id = lax.broadcasted_iota(jnp.int32, (SEGS, HEAD_DIM), 0)

    def scale_qk(i, marks):
        rows = pl.ds(pl.multiple_of(i * SEG, SEG), SEG)
        rows_copy(q_hbm, q_v, q_sem, i).wait()
        rows_copy(k_hbm, k_v, k_sem, i).wait()
        following = []
        for n in range(2 * HEADS):
            buf, h = (q_v, n) if n < HEADS else (k_v, n - HEADS)
            x = (buf[rows, cols(h)].astype(F32) * sc_qk[rows, n : n + 1]).astype(BF16)
            buf[rows, cols(h)] = x
            mean = jnp.sum(x.astype(F32), axis=0, keepdims=True) * (1.0 / SEG)
            following.append(jnp.where(seg_id == i, mean, marks[n]))
        return tuple(following)

    marks = lax.fori_loop(
        0, SEGS, scale_qk, (jnp.zeros((SEGS, HEAD_DIM), F32),) * (2 * HEADS)
    )
    for h in range(HEADS):
        both = jnp.concatenate([marks[h], marks[HEADS + h]], axis=0)
        lm_all[me, :, cols(h)] = both.astype(BF16)

    pl.semaphore_wait(barrier, SEQN - 1 + HEADN - 1)


    def lm_copy(r, slot):
        return pltpu.make_async_remote_copy(
            src_ref=lm_all.at[slot],
            dst_ref=lm_all.at[slot],
            send_sem=lm_s.at[r],
            recv_sem=lm_r.at[slot],
            device_id=(partner(r), zme),
            device_id_type=MESH,
        )

    def send_lm(r, _):
        lm_copy(r, me).start()
        return 0

    lax.fori_loop(1, SEQN, send_lm, 0)

    def scale_v(i, _):
        rows = pl.ds(pl.multiple_of(i * SEG, SEG), SEG)
        out_rows = pl.ds(pl.multiple_of(i * SEG + REACH, REACH), SEG)
        rows_copy(v_hbm, v_raw, v_sem, i).wait()
        for h in range(HEADS):
            x = (v_raw[rows, cols(h)].astype(F32) * sc_v[rows, h : h + 1]).astype(BF16)
            v_pad[out_rows, cols(h)] = x
            vt[h, :, rows] = x.astype(F32).T.astype(BF16)
        return 0

    lax.fori_loop(0, SEGS, scale_v, 0, unroll=2)
    v_pad[TOK + 2 * REACH :, :] = jnp.zeros((128 - 2 * REACH, WIDTH), BF16)

    after, before = (me + 1) % SEQN, (me + SEQN - 1) % SEQN
    down = pltpu.make_async_remote_copy(
        src_ref=v_pad.at[pl.ds(TOK, REACH)],
        dst_ref=v_pad.at[pl.ds(0, REACH)],
        send_sem=halo_s.at[0],
        recv_sem=halo_r.at[0],
        device_id=(after, zme),
        device_id_type=MESH,
    )
    up = pltpu.make_async_remote_copy(
        src_ref=v_pad.at[pl.ds(REACH, REACH)],
        dst_ref=v_pad.at[pl.ds(TOK + REACH, REACH)],
        send_sem=halo_s.at[1],
        recv_sem=halo_r.at[1],
        device_id=(before, zme),
        device_id_type=MESH,
    )
    down.start()
    up.start()

    wpad[...] = jnp.zeros_like(wpad)
    wpad[0:HEADS, 0:TAPS] = taps[...]
    for h in range(HEADS):
        line = jnp.broadcast_to(wpad[h : h + 1, :], (128, 256))
        toep[h] = pltpu.roll(line, 0, 1, stride=1, stride_axis=0).astype(BF16)

    def conv_block(b):
        window = pl.ds(pl.multiple_of(b * 128, 128), 256)
        rows = pl.ds(pl.multiple_of(b * 128, 128), 128)
        for h in range(HEADS):
            conv[rows, cols(h)] = dot(toep[h], v_pad[window, cols(h)])

    def conv_inner(b, _):
        conv_block(b)
        return 0

    lax.fori_loop(1, TOK // 128 - 1, conv_inner, 0, unroll=2)

    def recv_lm(r, _):
        lm_copy(r, partner(r)).wait_recv()
        return 0

    lax.fori_loop(1, SEQN, recv_lm, 0)
    for h in range(HEADS):
        both = lm_all[:, :, cols(h)].astype(F32)
        qm[h] = both[:, :SEGS].reshape(LANDMARKS, HEAD_DIM).astype(BF16)
        keys = both[:, SEGS:].reshape(LANDMARKS, HEAD_DIM)
        km[h] = keys.astype(BF16)
        kmt[h] = keys.T.astype(BF16)

    col_top = jnp.zeros((1, 1), F32)
    row_top = jnp.zeros((1, 1), F32)
    for h in range(HEADS):
        s = dot(qm[h], kmt[h])
        e = jnp.exp2((s - jnp.max(s, axis=1, keepdims=True)) * SCALE2)
        m = e / jnp.sum(e, axis=1, keepdims=True)
        mid[h] = m
        c = jnp.sum(m, axis=0, keepdims=True)
        r = jnp.sum(m, axis=1, keepdims=True)
        col_top = jnp.maximum(col_top, jnp.max(c, axis=1, keepdims=True))
        row_top = jnp.maximum(row_top, jnp.max(r, axis=0, keepdims=True))
    first_half = lax.broadcasted_iota(jnp.int32, (8, 128), 0) < 4
    tops[zme] = jnp.where(
        first_half, jnp.broadcast_to(col_top, (8, 128)), jnp.broadcast_to(row_top, (8, 128))
    )

    def top_copy(r, slot):
        return pltpu.make_async_remote_copy(
            src_ref=tops.at[slot],
            dst_ref=tops.at[slot],
            send_sem=top_s.at[r],
            recv_sem=top_r.at[slot],
            device_id=(me, (zme + r) % HEADN),
            device_id_type=MESH,
        )

    def send_top(r, _):
        top_copy(r, zme).start()
        return 0

    lax.fori_loop(1, HEADN, send_top, 0)

    def rs_copy(block, slot, target):
        return pltpu.make_async_remote_copy(
            src_ref=rs_send.at[block],
            dst_ref=rs_recv.at[slot],
            send_sem=rs_s.at[block],
            recv_sem=rs_r.at[slot],
            device_id=(target, zme),
            device_id_type=MESH,
        )

    row_id = lax.broadcasted_iota(jnp.int32, (SLICE, 128), 0)
    for h in range(HEADS):
        def far_scores(i, top):
            rows = pl.ds(pl.multiple_of(i * SEG, SEG), SEG)
            s = dot_nt(k_v[rows, cols(h)], qm[h])
            score[rows, :] = s
            return jnp.maximum(top, jnp.max(s.reshape(SEG // 8, 8, LANDMARKS), axis=0))

        top = lax.fori_loop(
            0, SEGS, far_scores, jnp.full((8, LANDMARKS), -jnp.inf, F32), unroll=True
        )
        top = jnp.max(top, axis=0, keepdims=True).astype(BF16).astype(F32)

        def far_weights(i, total):
            rows = pl.ds(pl.multiple_of(i * SEG, SEG), SEG)
            e = jnp.exp2((score[rows, :] - top) * SCALE2)
            wt[rows, :] = e.astype(BF16)
            return total + jnp.sum(e.reshape(SEG // 8, 8, LANDMARKS), axis=0)

        total = lax.fori_loop(
            0, SEGS, far_weights, jnp.zeros((8, LANDMARKS), F32), unroll=True
        )
        total = jnp.sum(total, axis=0, keepdims=True)
        total_hi = total.astype(BF16).astype(F32)
        total_lo = total - total_hi
        summed = dot(vt[h], wt[...])
        facts = jnp.zeros((SLICE, 128), F32)
        for n, (vec, half) in enumerate(
            (v, half) for v in (top, total_hi, total_lo) for half in range(2)
        ):
            part = jnp.broadcast_to(vec[:, half * 128 : (half + 1) * 128], (SLICE, 128))
            facts = jnp.where(row_id == n, part, facts)
        rs_send[h * OWN : (h + 1) * OWN, :, 0:LANDMARKS] = (
            summed.astype(BF16).reshape(OWN, SLICE, LANDMARKS)
        )
        rs_send[h * OWN : (h + 1) * OWN, :, LANDMARKS:PACK] = jnp.broadcast_to(
            facts.astype(BF16)[None], (OWN, SLICE, 128)
        )

        def send_rs(n, _):
            j = (n + j_me) % OWN
            target = owner(h, j)
            block = h * OWN + j

            @pl.when(target != me)
            def _():
                rs_copy(block, me, target).start()

            return 0

        lax.fori_loop(0, OWN, send_rs, 0)
    rs_recv[me] = rs_send[b_me]

    down.wait_recv()
    up.wait_recv()
    v_pad[0:REACH, :] = jnp.where(me == 0, jnp.zeros((REACH, WIDTH), BF16), v_pad[0:REACH, :])
    v_pad[TOK + REACH : TOK + 2 * REACH, :] = jnp.where(
        me == SEQN - 1, jnp.zeros((REACH, WIDTH), BF16), v_pad[TOK + REACH : TOK + 2 * REACH, :]
    )
    conv_block(0)
    conv_block(TOK // 128 - 1)

    def recv_top(r, _):
        top_copy(r, (zme + r) % HEADN).wait_recv()
        return 0

    lax.fori_loop(1, HEADN, recv_top, 0)

    best = jnp.max(tops[...], axis=0)
    scale = 1.0 / (best[0:1, 0:1] * best[4:5, 0:1])
    m = mid[h_me]
    mb = m.astype(BF16)
    x_ref[0:LANDMARKS, :] = dot(m.T.astype(BF16), mb) * scale
    x_ref[LANDMARKS:, :] = m * scale

    def sweep(_, carry):
        x = x_ref[...]
        xb = x.astype(BF16)
        y = dot(xb, xb[:LANDMARKS])
        b = (7.0 * x[:LANDMARKS] - y[:LANDMARKS]).astype(BF16)
        x_ref[...] = 0.25 * (13.0 * x - 15.0 * y + dot(y.astype(BF16), b))
        return carry

    lax.fori_loop(0, SWEEPS, sweep, 0)

    def near_softmax(i, _):
        rows = pl.ds(pl.multiple_of(i * SEG, SEG), SEG)
        for h in range(HEADS):
            s = dot(q_v[rows, cols(h)], kmt[h])
            e = jnp.exp2((s - jnp.max(s, axis=1, keepdims=True)) * SCALE2)
            near[h, rows, :] = (e * (1.0 / jnp.sum(e, axis=1, keepdims=True))).astype(BF16)
        return 0

    lax.fori_loop(0, NEAR_EARLY, near_softmax, 0)

    def recv_rs(r, _):
        rs_copy(0, partner(r), me).wait_recv()
        return 0

    lax.fori_loop(1, SEQN, recv_rs, 0)


    def facts_top(s, top):
        return jnp.maximum(top, rs_recv[s, :, LANDMARKS:PACK].astype(F32))

    top = lax.fori_loop(0, SEQN, facts_top, jnp.full((SLICE, 128), -jnp.inf, F32))

    def combine(s, carry):
        num, den = carry
        facts = rs_recv[s, :, LANDMARKS:PACK].astype(F32)
        e = jnp.exp2((facts - top) * SCALE2)
        w = jnp.concatenate([e[0:1], e[1:2]], axis=1)
        part = jnp.concatenate([facts[2:3] + facts[4:5], facts[3:4] + facts[5:6]], axis=1)
        return num + rs_recv[s, :, 0:LANDMARKS].astype(F32) * w, den + part * w

    num, den = lax.fori_loop(
        0, SEQN, combine, (jnp.zeros((SLICE, LANDMARKS), F32), jnp.zeros((1, LANDMARKS), F32))
    )
    reduced = (num / den).astype(BF16)
    mp_all[b_me] = dot(reduced, x_ref[LANDMARKS:, :].astype(BF16)).astype(BF16)

    def mp_copy(r, slot):
        return pltpu.make_async_remote_copy(
            src_ref=mp_all.at[slot],
            dst_ref=mp_all.at[slot],
            send_sem=mp_s.at[r],
            recv_sem=mp_r.at[slot],
            device_id=(partner(r), zme),
            device_id_type=MESH,
        )

    def send_mp(r, _):
        mp_copy(r, b_me).start()
        return 0

    lax.fori_loop(1, SEQN, send_mp, 0)

    lax.fori_loop(NEAR_EARLY, SEGS, near_softmax, 0)


    for h in range(HEADS):
        for j in range(OWN):
            b = h * OWN + j

            @pl.when(b != b_me)
            def _():
                mp_copy(0, b).wait_recv()

    mapped = [
        mp_all[h * OWN : (h + 1) * OWN].reshape(HEAD_DIM, LANDMARKS).astype(F32).T.astype(BF16)
        for h in range(HEADS)
    ]
    step = 512
    for i in range(TOK // step):
        rows = slice(i * step, (i + 1) * step)
        for h in range(HEADS):
            out_v[rows, cols(h)] = (dot(near[h, rows, :], mapped[h]) + conv[rows, cols(h)]).astype(
                BF16
            )
        pltpu.make_async_copy(out_v.at[rows], out_hbm.at[rows], out_sem.at[i]).start()

    down.wait_send()
    up.wait_send()

    def sent(r, _):
        lm_copy(r, me).wait_send()
        mp_copy(r, b_me).wait_send()
        return 0

    lax.fori_loop(1, SEQN, sent, 0)

    def sent_top(r, _):
        top_copy(r, zme).wait_send()
        return 0

    lax.fori_loop(1, HEADN, sent_top, 0)

    def sent_rs(b, _):
        @pl.when(b != b_me)
        def _():
            rs_copy(b, me, me).wait_send()

        return 0

    lax.fori_loop(0, SEQN, sent_rs, 0)
    for i in range(TOK // step):
        rows = slice(i * step, (i + 1) * step)
        pltpu.make_async_copy(out_v.at[rows], out_hbm.at[rows], out_sem.at[i]).wait()


def shards(q, k, v, qs, ks, vs, cw):
    dma = pltpu.SemaphoreType.DMA
    vm = pltpu.VMEM
    hbm = pl.BlockSpec(memory_space=pl.ANY)
    return pl.pallas_call(
        kernel,
        out_shape=jax.ShapeDtypeStruct((TOK, WIDTH), BF16),
        in_specs=[hbm] * 7,
        out_specs=hbm,
        scratch_shapes=[
            vm((3, HEADS, TOK), F32),
            vm((HEADS, TAPS), F32),
            vm((TOK, WIDTH), BF16),
            vm((TOK, WIDTH), BF16),
            vm((TOK, WIDTH), BF16),
            vm((TOK + 128, WIDTH), BF16),
            vm((HEADS, HEAD_DIM, TOK), BF16),
            vm((TOK, 8), F32),
            vm((TOK, 8), F32),
            vm((SEQN, 2 * SEGS, WIDTH), BF16),
            vm((HEADS, LANDMARKS, HEAD_DIM), BF16),
            vm((HEADS, LANDMARKS, HEAD_DIM), BF16),
            vm((HEADS, HEAD_DIM, LANDMARKS), BF16),
            vm((HEADS, LANDMARKS, LANDMARKS), F32),
            vm((HEADN, 8, 128), F32),
            vm((TOK, LANDMARKS), F32),
            vm((TOK, LANDMARKS), BF16),
            vm((SEQN, SLICE, PACK), BF16),
            vm((SEQN, SLICE, PACK), BF16),
            vm((2 * LANDMARKS, LANDMARKS), F32),
            vm((HEADS, TOK, LANDMARKS), BF16),
            vm((TOK, WIDTH), F32),
            vm((SEQN, SLICE, LANDMARKS), BF16),
            vm((TOK, WIDTH), BF16),
            vm((8, 256), F32),
            vm((HEADS, 128, 256), BF16),
            dma((4,)),
            dma((SEGS,)),
            dma((SEGS,)),
            dma((SEGS,)),
            dma((4,)),
            dma((SEQN,)),
            dma((SEQN,)),
            dma((2,)),
            dma((2,)),
            dma((HEADN,)),
            dma((HEADN,)),
            dma((SEQN,)),
            dma((SEQN,)),
            dma((SEQN,)),
            dma((SEQN,)),
        ],
        compiler_params=pltpu.CompilerParams(
            collective_id=0, has_side_effects=True, vmem_limit_bytes=62 * 1024 * 1024
        ),
        name="nystrom",
    )(q, k, v, qs.T, ks.T, vs.T, cw)


def solution(mesh):
    tokens, heads = P("seq", "head"), P("head", None)
    return jax.shard_map(
        shards, mesh=mesh, in_specs=(tokens,) * 6 + (heads,), out_specs=tokens, check_vma=False
    )
```

```python
import functools
import math

import jax
import jax.numpy as jnp
from jax import lax
from jax.experimental import pallas as pl
from jax.experimental.pallas import tpu as pltpu
from jax.sharding import PartitionSpec as P

MESH = pl.DeviceIdType.MESH
F32 = jnp.float32
BF16 = jnp.bfloat16
HEAD_DIM = 128
LANDMARKS = 256
SWEEPS = 6
TAPS = 33
REACH = TAPS // 2
LOG2E = math.log2(math.e)
SCALE2 = HEAD_DIM**-0.5 * LOG2E
FACTOR = HEAD_DIM**-0.5

TOK = 2048
HEADS = 4
WIDTH = HEADS * HEAD_DIM
SEQN = 32
HEADN = 8
SEGS = 8
SEG = 256
CHIPS = SEQN // 2
OWN = 8
SLICE = HEAD_DIM // OWN
PACK = LANDMARKS + 128
NEAR_EARLY = 4


def dot(a, b):
    return jnp.dot(a, b, preferred_element_type=F32)


def dot_nt(a, b):
    return lax.dot_general(a, b, (((1,), (1,)), ((), ())), preferred_element_type=F32)


def cols(h):
    return slice(h * HEAD_DIM, (h + 1) * HEAD_DIM)


def kernel(
    q_hbm, k_hbm, v_hbm, small, out,
    q_v, k_v, v_raw, v_pad, vt, sc_qk, sc_v, lm_all, qm, km, kmt,
    mid, tops, score, wt, rs_send, rs_recv, x_ref, near, conv, mp_all, toep,
    q_sem, k_sem, v_sem, lm_s, lm_r, halo_s, halo_r, top_s, top_r, rs_s, rs_r, mp_s, mp_r,
):
    me = lax.axis_index("seq")
    zme = lax.axis_index("head")
    yme, xme, cme = me // 8, (me // 2) % 4, me % 2
    h_me = 2 * ((xme + yme) % 2) + cme
    j_me = (me // 2) // 2
    chip = me // 2
    other = me + 1 - 2 * cme

    def partner(r):
        return (
            ((yme + r // 8) % 4) * 8 + ((xme + (r // 2) % 4) % 4) * 2 + (cme + r % 2) % 2
        )

    def across(r):
        return ((yme + r // 4) % 4) * 8 + ((xme + r % 4) % 4) * 2 + cme

    def owner(h, j):
        y = j // 2
        return (4 * y + 2 * (j % 2) + (h // 2 + y) % 2) * 2 + h % 2

    def rows_copy(src, dst, sem, i):
        rows = pl.ds(i * SEG, SEG)
        return pltpu.make_async_copy(src.at[rows], dst.at[rows], sem.at[i])

    for i in range(SEGS):
        rows_copy(q_hbm, q_v, q_sem, i).start()
        rows_copy(k_hbm, k_v, k_sem, i).start()

    barrier = pltpu.get_barrier_semaphore()

    def greet_seq(r, _):
        pl.semaphore_signal(barrier, inc=1, device_id=(partner(r), zme), device_id_type=MESH)
        return 0

    def greet_head(r, _):
        pl.semaphore_signal(
            barrier, inc=1, device_id=(me, (zme + r) % HEADN), device_id_type=MESH
        )
        return 0

    lax.fori_loop(1, SEQN, greet_seq, 0)
    lax.fori_loop(1, HEADN, greet_head, 0)

    sc_qk[...] = small[0 : 2 * HEADS, :].T
    sc_v[...] = small[2 * HEADS : 4 * HEADS, :].T

    seg_id = lax.broadcasted_iota(jnp.int32, (SEGS, HEAD_DIM), 0)

    def scale_qk(i, marks):
        rows = pl.ds(pl.multiple_of(i * SEG, SEG), SEG)
        rows_copy(q_hbm, q_v, q_sem, i).wait()
        rows_copy(k_hbm, k_v, k_sem, i).wait()
        rows_copy(v_hbm, v_raw, v_sem, i).start()
        following = []
        for n in range(2 * HEADS):
            buf, h = (q_v, n) if n < HEADS else (k_v, n - HEADS)
            x = (buf[rows, cols(h)].astype(F32) * sc_qk[rows, n : n + 1]).astype(BF16)
            buf[rows, cols(h)] = x
            mean = jnp.sum(x.astype(F32), axis=0, keepdims=True) * (1.0 / SEG)
            following.append(jnp.where(seg_id == i, mean, marks[n]))
        return tuple(following)

    marks = lax.fori_loop(
        0, SEGS, scale_qk, (jnp.zeros((SEGS, HEAD_DIM), F32),) * (2 * HEADS)
    )
    for h in range(HEADS):
        both = jnp.concatenate([marks[h], marks[HEADS + h]], axis=0)
        lm_all[cme, chip, :, cols(h)] = both.astype(BF16)

    pl.semaphore_wait(barrier, SEQN - 1 + HEADN - 1)

    def group_copy(buf, at, sems, n, target):
        return pltpu.make_async_remote_copy(
            src_ref=buf.at[at],
            dst_ref=buf.at[at],
            send_sem=sems[0].at[n],
            recv_sem=sems[1].at[n],
            device_id=(target, zme),
            device_id_type=MESH,
        )

    for r in range(1, CHIPS):
        group_copy(lm_all, (cme, chip), (lm_s, lm_r), 0, across(r)).start()
    lm_total = group_copy(lm_all, (0, pl.ds(0, CHIPS - 1)), (lm_s, lm_r), 0, other)
    lm_out = group_copy(lm_all, (cme,), (lm_s, lm_r), 1, other)
    lm_in = group_copy(lm_all, (1 - cme,), (lm_s, lm_r), 1, other)

    def scale_v(i, _):
        rows = pl.ds(pl.multiple_of(i * SEG, SEG), SEG)
        out_rows = pl.ds(pl.multiple_of(i * SEG + REACH, REACH), SEG)
        rows_copy(v_hbm, v_raw, v_sem, i).wait()
        for h in range(HEADS):
            x = (v_raw[rows, cols(h)].astype(F32) * sc_v[rows, h : h + 1]).astype(BF16)
            v_pad[out_rows, cols(h)] = x
            vt[h, :, rows] = x.astype(F32).T.astype(BF16)
        return 0

    lax.fori_loop(0, SEGS, scale_v, 0, unroll=2)
    v_pad[TOK + 2 * REACH :, :] = jnp.zeros((128 - 2 * REACH, WIDTH), BF16)

    after, before = (me + 1) % SEQN, (me + SEQN - 1) % SEQN
    down = pltpu.make_async_remote_copy(
        src_ref=v_pad.at[pl.ds(TOK, REACH)],
        dst_ref=v_pad.at[pl.ds(0, REACH)],
        send_sem=halo_s.at[0],
        recv_sem=halo_r.at[0],
        device_id=(after, zme),
        device_id_type=MESH,
    )
    up = pltpu.make_async_remote_copy(
        src_ref=v_pad.at[pl.ds(REACH, REACH)],
        dst_ref=v_pad.at[pl.ds(TOK + REACH, REACH)],
        send_sem=halo_s.at[1],
        recv_sem=halo_r.at[1],
        device_id=(before, zme),
        device_id_type=MESH,
    )
    down.start()
    up.start()

    for h in range(HEADS):
        line = jnp.broadcast_to(small[3 * HEADS + h : 3 * HEADS + h + 1, 0:256], (128, 256))
        toep[h] = pltpu.roll(line, 0, 1, stride=1, stride_axis=0).astype(BF16)

    def conv_block(b):
        window = pl.ds(pl.multiple_of(b * 128, 128), 256)
        rows = pl.ds(pl.multiple_of(b * 128, 128), 128)
        for h in range(HEADS):
            conv[rows, cols(h)] = dot(toep[h], v_pad[window, cols(h)])

    def conv_inner(b, _):
        conv_block(b)
        return 0

    lax.fori_loop(1, TOK // 128 - 1, conv_inner, 0, unroll=2)

    lm_total.wait_recv()
    lm_out.start()

    lm_in.wait_recv()

    for h in range(HEADS):
        both = lm_all[:, :, :, cols(h)].reshape(SEQN, 2 * SEGS, HEAD_DIM).astype(F32)
        qm[h] = both[:, :SEGS].reshape(LANDMARKS, HEAD_DIM).astype(BF16)
        keys = both[:, SEGS:].reshape(LANDMARKS, HEAD_DIM)
        km[h] = keys.astype(BF16)
        kmt[h] = keys.T.astype(BF16)

    col_top = jnp.zeros((1, 1), F32)
    row_top = jnp.zeros((1, 1), F32)
    for h in range(HEADS):
        s = dot(qm[h], kmt[h])
        e = jnp.exp2((s - jnp.max(s, axis=1, keepdims=True)) * SCALE2)
        m = e / jnp.sum(e, axis=1, keepdims=True)
        mid[h] = m
        c = jnp.sum(m, axis=0, keepdims=True)
        r = jnp.sum(m, axis=1, keepdims=True)
        col_top = jnp.maximum(col_top, jnp.max(c, axis=1, keepdims=True))
        row_top = jnp.maximum(row_top, jnp.max(r, axis=0, keepdims=True))
    first_half = lax.broadcasted_iota(jnp.int32, (8, 128), 0) < 4
    tops[zme] = jnp.where(
        first_half, jnp.broadcast_to(col_top, (8, 128)), jnp.broadcast_to(row_top, (8, 128))
    )

    def top_copy(at, target):
        return pltpu.make_async_remote_copy(
            src_ref=tops.at[at],
            dst_ref=tops.at[at],
            send_sem=top_s.at[0],
            recv_sem=top_r.at[0],
            device_id=(me, target),
            device_id_type=MESH,
        )

    for r in range(1, HEADN):
        top_copy(zme, (zme + r) % HEADN).start()
    top_total = top_copy(pl.ds(0, HEADN - 1), zme)

    def rs_copy(block, slot, target):
        return pltpu.make_async_remote_copy(
            src_ref=rs_send.at[block],
            dst_ref=rs_recv.at[slot],
            send_sem=rs_s.at[0],
            recv_sem=rs_r.at[0],
            device_id=(target, zme),
            device_id_type=MESH,
        )

    row_id = lax.broadcasted_iota(jnp.int32, (SLICE, 128), 0)
    for h in range(HEADS):
        def far_scores(i, top):
            rows = pl.ds(pl.multiple_of(i * SEG, SEG), SEG)
            s = dot_nt(k_v[rows, cols(h)], qm[h])
            score[rows, :] = s
            return jnp.maximum(top, jnp.max(s.reshape(SEG // 8, 8, LANDMARKS), axis=0))

        top = lax.fori_loop(
            0, SEGS, far_scores, jnp.full((8, LANDMARKS), -jnp.inf, F32), unroll=True
        )
        top = jnp.max(top, axis=0, keepdims=True).astype(BF16).astype(F32)

        def far_weights(i, total):
            rows = pl.ds(pl.multiple_of(i * SEG, SEG), SEG)
            e = jnp.exp2((score[rows, :] - top) * SCALE2)
            wt[rows, :] = e.astype(BF16)
            return total + jnp.sum(e.reshape(SEG // 8, 8, LANDMARKS), axis=0)

        total = lax.fori_loop(
            0, SEGS, far_weights, jnp.zeros((8, LANDMARKS), F32), unroll=True
        )
        total = jnp.sum(total, axis=0, keepdims=True)
        total_hi = total.astype(BF16).astype(F32)
        total_lo = total - total_hi
        summed = dot(vt[h], wt[...])
        facts = jnp.zeros((SLICE, 128), F32)
        for n, (vec, half) in enumerate(
            (v, half) for v in (top, total_hi, total_lo) for half in range(2)
        ):
            part = jnp.broadcast_to(vec[:, half * 128 : (half + 1) * 128], (SLICE, 128))
            facts = jnp.where(row_id == n, part, facts)
        rs_send[h * OWN : (h + 1) * OWN, :, 0:LANDMARKS] = (
            summed.astype(BF16).reshape(OWN, SLICE, LANDMARKS)
        )
        rs_send[h * OWN : (h + 1) * OWN, :, LANDMARKS:PACK] = jnp.broadcast_to(
            facts.astype(BF16)[None], (OWN, SLICE, 128)
        )


    for h in range(HEADS):
        for n in range(1, OWN):
            j = (n + j_me) % OWN
            rs_copy(h * OWN + j, me, owner(h, j)).start()
    for n in range(1, HEADS):
        h = (h_me + n) % HEADS
        rs_copy(h * OWN + j_me, me, owner(h, j_me)).start()
    rs_total = rs_copy(pl.ds(0, SEQN - 1), pl.ds(0, SEQN - 1), other)
    rs_recv[me] = rs_send[h_me * OWN + j_me]

    down.wait_recv()
    up.wait_recv()
    v_pad[0:REACH, :] = jnp.where(me == 0, jnp.zeros((REACH, WIDTH), BF16), v_pad[0:REACH, :])
    v_pad[TOK + REACH : TOK + 2 * REACH, :] = jnp.where(
        me == SEQN - 1, jnp.zeros((REACH, WIDTH), BF16), v_pad[TOK + REACH : TOK + 2 * REACH, :]
    )
    conv_block(0)
    conv_block(TOK // 128 - 1)

    def near_softmax(i, _):
        rows = pl.ds(pl.multiple_of(i * SEG, SEG), SEG)
        for h in range(HEADS):
            s = dot(q_v[rows, cols(h)], kmt[h])
            e = jnp.exp2((s - jnp.max(s, axis=1, keepdims=True)) * SCALE2)
            near[h, rows, :] = (e * (1.0 / jnp.sum(e, axis=1, keepdims=True))).astype(BF16)
        return 0

    lax.fori_loop(0, NEAR_EARLY, near_softmax, 0)

    top_total.wait_recv()

    best = jnp.max(tops[...], axis=0)
    scale = 1.0 / (best[0:1, 0:1] * best[4:5, 0:1])
    m = mid[h_me]
    mb = m.astype(BF16)
    x_ref[0:LANDMARKS, :] = dot(m.T.astype(BF16), mb) * scale
    x_ref[LANDMARKS:, :] = m * scale

    def sweep(_, carry):
        x = x_ref[...]
        xb = x.astype(BF16)
        y = dot(xb, xb[:LANDMARKS])
        b = (7.0 * x[:LANDMARKS] - y[:LANDMARKS]).astype(BF16)
        x_ref[...] = 0.25 * (13.0 * x - 15.0 * y + dot(y.astype(BF16), b))
        return carry

    lax.fori_loop(0, SWEEPS, sweep, 0)

    rs_total.wait_recv()


    def facts_top(s, top):
        return jnp.maximum(top, rs_recv[s, :, LANDMARKS:PACK].astype(F32))

    top = lax.fori_loop(0, SEQN, facts_top, jnp.full((SLICE, 128), -jnp.inf, F32))

    def combine(s, carry):
        num, den = carry
        facts = rs_recv[s, :, LANDMARKS:PACK].astype(F32)
        e = jnp.exp2((facts - top) * SCALE2)
        w = jnp.concatenate([e[0:1], e[1:2]], axis=1)
        part = jnp.concatenate([facts[2:3] + facts[4:5], facts[3:4] + facts[5:6]], axis=1)
        return num + rs_recv[s, :, 0:LANDMARKS].astype(F32) * w, den + part * w

    num, den = lax.fori_loop(
        0, SEQN, combine, (jnp.zeros((SLICE, LANDMARKS), F32), jnp.zeros((1, LANDMARKS), F32))
    )
    reduced = (num / den).astype(BF16)
    slot = (h_me // 2) * OWN + j_me
    mp_all[cme, slot] = dot(reduced, x_ref[LANDMARKS:, :].astype(BF16)).astype(BF16)
    for r in range(1, CHIPS):
        group_copy(mp_all, (cme, slot), (mp_s, mp_r), 0, across(r)).start()
    mp_total = group_copy(mp_all, (0, pl.ds(0, CHIPS - 1)), (mp_s, mp_r), 0, other)
    mp_out = group_copy(mp_all, (cme,), (mp_s, mp_r), 1, other)
    mp_in = group_copy(mp_all, (1 - cme,), (mp_s, mp_r), 1, other)

    lax.fori_loop(NEAR_EARLY, SEGS, near_softmax, 0)

    mp_total.wait_recv()
    mp_out.start()

    def attend(h):
        lanes = pl.ds(pl.multiple_of(h * HEAD_DIM, HEAD_DIM), HEAD_DIM)
        mapped = mp_all[h % 2, pl.ds((h // 2) * OWN, OWN)].reshape(HEAD_DIM, LANDMARKS).astype(F32).T.astype(BF16)
        for i in range(4):
            rows = slice(i * 512, (i + 1) * 512)
            out[rows, lanes] = (dot(near[h, rows, :], mapped) + conv[rows, lanes]).astype(BF16)

    attend(cme)
    attend(cme + 2)

    mp_in.wait_recv()

    attend(1 - cme)
    attend(3 - cme)

    down.wait_send()
    up.wait_send()
    lm_total.wait_send()
    lm_out.wait_send()
    top_total.wait_send()
    rs_total.wait_send()
    mp_total.wait_send()
    mp_out.wait_send()


def shards(q, k, v, qs, ks, vs, cw):
    dma = pltpu.SemaphoreType.DMA
    vm = pltpu.VMEM
    hbm = pl.BlockSpec(memory_space=pl.ANY)
    whole = pl.BlockSpec(memory_space=pltpu.VMEM)
    taps = jnp.pad(cw, ((0, 0), (0, TOK - TAPS)))
    small = jnp.concatenate([qs.T, ks.T, vs.T, taps], axis=0)
    return pl.pallas_call(
        kernel,
        out_shape=jax.ShapeDtypeStruct((TOK, WIDTH), BF16),
        in_specs=[hbm, hbm, hbm, whole],
        out_specs=whole,
        scratch_shapes=[
            vm((TOK, WIDTH), BF16),
            vm((TOK, WIDTH), BF16),
            vm((TOK, WIDTH), BF16),
            vm((TOK + 128, WIDTH), BF16),
            vm((HEADS, HEAD_DIM, TOK), BF16),
            vm((TOK, 8), F32),
            vm((TOK, 8), F32),
            vm((2, CHIPS, 2 * SEGS, WIDTH), BF16),
            vm((HEADS, LANDMARKS, HEAD_DIM), BF16),
            vm((HEADS, LANDMARKS, HEAD_DIM), BF16),
            vm((HEADS, HEAD_DIM, LANDMARKS), BF16),
            vm((HEADS, LANDMARKS, LANDMARKS), F32),
            vm((HEADN, 8, 128), F32),
            vm((TOK, LANDMARKS), F32),
            vm((TOK, LANDMARKS), BF16),
            vm((SEQN, SLICE, PACK), BF16),
            vm((SEQN, SLICE, PACK), BF16),
            vm((2 * LANDMARKS, LANDMARKS), F32),
            vm((HEADS, TOK, LANDMARKS), BF16),
            vm((TOK, WIDTH), F32),
            vm((2, CHIPS, SLICE, LANDMARKS), BF16),
            vm((HEADS, 128, 256), BF16),
            dma((SEGS,)),
            dma((SEGS,)),
            dma((SEGS,)),
            dma((2,)),
            dma((2,)),
            dma((2,)),
            dma((2,)),
            dma((1,)),
            dma((1,)),
            dma((1,)),
            dma((1,)),
            dma((2,)),
            dma((2,)),
        ],
        compiler_params=pltpu.CompilerParams(
            collective_id=0, has_side_effects=True, vmem_limit_bytes=50 * 1024 * 1024
        ),
        name="nystrom",
    )(q, k, v, small)


def solution(mesh):
    tokens, heads = P("seq", "head"), P("head", None)
    return jax.shard_map(
        shards, mesh=mesh, in_specs=(tokens,) * 6 + (heads,), out_specs=tokens, check_vma=False
    )
```

```python
import functools
import math

import jax
import jax.numpy as jnp
from jax import lax
from jax.experimental import pallas as pl
from jax.experimental.pallas import tpu as pltpu
from jax.sharding import PartitionSpec as P

MESH = pl.DeviceIdType.MESH
F32 = jnp.float32
BF16 = jnp.bfloat16
HEAD_DIM = 128
LANDMARKS = 256
SWEEPS = 6
TAPS = 33
REACH = TAPS // 2
LOG2E = math.log2(math.e)
SCALE2 = HEAD_DIM**-0.5 * LOG2E
FACTOR = HEAD_DIM**-0.5

TOK = 2048
HEADS = 4
WIDTH = HEADS * HEAD_DIM
SEQN = 32
HEADN = 8
SEGS = 8
SEG = 256
CHIPS = SEQN // 2
OWN = 8
SLICE = HEAD_DIM // OWN
PACK = LANDMARKS + 128
NEAR_EARLY = 4
CONV_SPLIT = 8


def dot(a, b):
    return jnp.dot(a, b, preferred_element_type=F32)


def dot_nt(a, b):
    return lax.dot_general(a, b, (((1,), (1,)), ((), ())), preferred_element_type=F32)


def cols(h):
    return slice(h * HEAD_DIM, (h + 1) * HEAD_DIM)


def kernel(
    q_hbm, k_hbm, v_hbm, small, out,
    q_v, k_v, v_raw, v_pad, vt, sc_qk, sc_v, lm_all, qm, km, kmt,
    mid, tops, score, wt, rs_send, rs_recv, x_ref, near, conv, mp_all, toep,
    q_sem, k_sem, v_sem, lm_s, lm_r, halo_s, halo_r, top_s, top_r, rs_s, rs_r, mp_s, mp_r, go_sem,
):
    me = lax.axis_index("seq")
    zme = lax.axis_index("head")
    yme, xme, cme = me // 8, (me // 2) % 4, me % 2
    h_me = 2 * ((xme + yme) % 2) + cme
    j_me = (me // 2) // 2
    chip = me // 2
    other = me + 1 - 2 * cme

    def partner(r):
        return (
            ((yme + r // 8) % 4) * 8 + ((xme + (r // 2) % 4) % 4) * 2 + (cme + r % 2) % 2
        )

    def across(r):
        return ((yme + r // 4) % 4) * 8 + ((xme + r % 4) % 4) * 2 + cme

    def owner(h, j):
        y = j // 2
        return (4 * y + 2 * (j % 2) + (h // 2 + y) % 2) * 2 + h % 2

    def rows_copy(src, dst, sem, i):
        rows = pl.ds(i * SEG, SEG)
        return pltpu.make_async_copy(src.at[rows], dst.at[rows], sem.at[i])

    for i in range(SEGS):
        rows_copy(q_hbm, q_v, q_sem, i).start()
        rows_copy(k_hbm, k_v, k_sem, i).start()

    barrier = pltpu.get_barrier_semaphore()

    def greet(r, _):
        target = ((yme + r // 4) % 4) * 8 + ((xme + r % 4) % 4) * 2
        pl.semaphore_signal(barrier, inc=1, device_id=(target, zme), device_id_type=MESH)
        return 0

    lax.fori_loop(1, CHIPS, greet, 0)

    @pl.when(cme == 1)
    def _():
        pl.semaphore_signal(barrier, inc=1, device_id=(other, zme), device_id_type=MESH)
        for r in range(1, HEADN):
            pl.semaphore_signal(
                barrier, inc=1, device_id=(me, (zme + r) % HEADN), device_id_type=MESH
            )

    sc_qk[...] = small[0 : 2 * HEADS, :].T
    sc_v[...] = small[2 * HEADS : 4 * HEADS, :].T

    seg_id = lax.broadcasted_iota(jnp.int32, (SEGS, HEAD_DIM), 0)

    def scale_qk(i, marks):
        rows = pl.ds(pl.multiple_of(i * SEG, SEG), SEG)
        rows_copy(q_hbm, q_v, q_sem, i).wait()
        rows_copy(k_hbm, k_v, k_sem, i).wait()
        rows_copy(v_hbm, v_raw, v_sem, i).start()
        following = []
        for n in range(2 * HEADS):
            buf, h = (q_v, n) if n < HEADS else (k_v, n - HEADS)
            x = (buf[rows, cols(h)].astype(F32) * sc_qk[rows, n : n + 1]).astype(BF16)
            buf[rows, cols(h)] = x
            mean = jnp.sum(x.astype(F32), axis=0, keepdims=True) * (1.0 / SEG)
            following.append(jnp.where(seg_id == i, mean, marks[n]))
        return tuple(following)

    marks = lax.fori_loop(
        0, SEGS, scale_qk, (jnp.zeros((SEGS, HEAD_DIM), F32),) * (2 * HEADS)
    )
    for h in range(HEADS):
        both = jnp.concatenate([marks[h], marks[HEADS + h]], axis=0)
        lm_all[cme, chip, :, cols(h)] = both.astype(BF16)

    @pl.when(cme == 0)
    def _():
        pl.semaphore_wait(barrier, SEQN - 1)
        pl.semaphore_signal(go_sem, inc=1, device_id=(other, zme), device_id_type=MESH)

    @pl.when(cme == 1)
    def _():
        pl.semaphore_wait(go_sem, 1)

    def group_copy(buf, at, sems, n, target):
        return pltpu.make_async_remote_copy(
            src_ref=buf.at[at],
            dst_ref=buf.at[at],
            send_sem=sems[0].at[n],
            recv_sem=sems[1].at[n],
            device_id=(target, zme),
            device_id_type=MESH,
        )

    for r in range(1, CHIPS):
        group_copy(lm_all, (cme, chip), (lm_s, lm_r), 0, across(r)).start()
    lm_total = group_copy(lm_all, (0, pl.ds(0, CHIPS - 1)), (lm_s, lm_r), 0, other)
    lm_out = group_copy(lm_all, (cme,), (lm_s, lm_r), 1, other)
    lm_in = group_copy(lm_all, (1 - cme,), (lm_s, lm_r), 1, other)

    def scale_v(i, _):
        rows = pl.ds(pl.multiple_of(i * SEG, SEG), SEG)
        out_rows = pl.ds(pl.multiple_of(i * SEG + REACH, REACH), SEG)
        rows_copy(v_hbm, v_raw, v_sem, i).wait()
        for h in range(HEADS):
            x = (v_raw[rows, cols(h)].astype(F32) * sc_v[rows, h : h + 1]).astype(BF16)
            v_pad[out_rows, cols(h)] = x
            vt[h, :, rows] = x.astype(F32).T.astype(BF16)
        return 0

    lax.fori_loop(0, SEGS, scale_v, 0, unroll=2)
    v_pad[TOK + 2 * REACH :, :] = jnp.zeros((128 - 2 * REACH, WIDTH), BF16)

    after, before = (me + 1) % SEQN, (me + SEQN - 1) % SEQN
    down = pltpu.make_async_remote_copy(
        src_ref=v_pad.at[pl.ds(TOK, REACH)],
        dst_ref=v_pad.at[pl.ds(0, REACH)],
        send_sem=halo_s.at[0],
        recv_sem=halo_r.at[0],
        device_id=(after, zme),
        device_id_type=MESH,
    )
    up = pltpu.make_async_remote_copy(
        src_ref=v_pad.at[pl.ds(REACH, REACH)],
        dst_ref=v_pad.at[pl.ds(TOK + REACH, REACH)],
        send_sem=halo_s.at[1],
        recv_sem=halo_r.at[1],
        device_id=(before, zme),
        device_id_type=MESH,
    )
    down.start()
    up.start()

    for h in range(HEADS):
        line = jnp.broadcast_to(small[3 * HEADS + h : 3 * HEADS + h + 1, 0:256], (128, 256))
        toep[h] = pltpu.roll(line, 0, 1, stride=1, stride_axis=0).astype(BF16)

    def conv_block(b):
        window = pl.ds(pl.multiple_of(b * 128, 128), 256)
        rows = pl.ds(pl.multiple_of(b * 128, 128), 128)
        for h in range(HEADS):
            conv[rows, cols(h)] = dot(toep[h], v_pad[window, cols(h)])

    def conv_inner(b, _):
        conv_block(b)
        return 0

    lax.fori_loop(1, CONV_SPLIT, conv_inner, 0, unroll=True)

    lm_total.wait_recv()
    lm_out.start()

    lax.fori_loop(CONV_SPLIT, TOK // 128 - 1, conv_inner, 0, unroll=True)

    lm_in.wait_recv()

    for h in range(HEADS):
        both = lm_all[:, :, :, cols(h)].reshape(SEQN, 2 * SEGS, HEAD_DIM).astype(F32)
        qm[h] = both[:, :SEGS].reshape(LANDMARKS, HEAD_DIM).astype(BF16)
        keys = both[:, SEGS:].reshape(LANDMARKS, HEAD_DIM)
        km[h] = keys.astype(BF16)
        kmt[h] = keys.T.astype(BF16)

    col_top = jnp.zeros((1, 1), F32)
    row_top = jnp.zeros((1, 1), F32)
    for h in range(HEADS):
        s = dot(qm[h], kmt[h])
        e = jnp.exp2((s - jnp.max(s, axis=1, keepdims=True)) * SCALE2)
        m = e / jnp.sum(e, axis=1, keepdims=True)
        mid[h] = m
        c = jnp.sum(m, axis=0, keepdims=True)
        r = jnp.sum(m, axis=1, keepdims=True)
        col_top = jnp.maximum(col_top, jnp.max(c, axis=1, keepdims=True))
        row_top = jnp.maximum(row_top, jnp.max(r, axis=0, keepdims=True))
    first_half = lax.broadcasted_iota(jnp.int32, (8, 128), 0) < 4
    own_top = jnp.where(
        first_half, jnp.broadcast_to(col_top, (8, 128)), jnp.broadcast_to(row_top, (8, 128))
    )

    @pl.when(cme == 1)
    def _():
        tops[zme] = own_top

    def top_copy(at, target):
        return pltpu.make_async_remote_copy(
            src_ref=tops.at[at],
            dst_ref=tops.at[at],
            send_sem=top_s.at[0],
            recv_sem=top_r.at[0],
            device_id=(me, target),
            device_id_type=MESH,
        )

    @pl.when(cme == 1)
    def _():
        pl.semaphore_wait(barrier, HEADN - 1)
        for r in range(1, HEADN):
            top_copy(zme, (zme + r) % HEADN).start()

    top_total = top_copy(pl.ds(0, HEADN - 1), zme)
    top_over = pltpu.make_async_remote_copy(
        src_ref=tops,
        dst_ref=tops,
        send_sem=top_s.at[1],
        recv_sem=top_r.at[1],
        device_id=(other, zme),
        device_id_type=MESH,
    )

    def rs_copy(block, slot, target):
        return pltpu.make_async_remote_copy(
            src_ref=rs_send.at[block],
            dst_ref=rs_recv.at[slot],
            send_sem=rs_s.at[0],
            recv_sem=rs_r.at[0],
            device_id=(target, zme),
            device_id_type=MESH,
        )

    row_id = lax.broadcasted_iota(jnp.int32, (SLICE, 128), 0)
    for h in range(HEADS):
        def far_scores(i, top):
            rows = pl.ds(pl.multiple_of(i * SEG, SEG), SEG)
            s = dot_nt(k_v[rows, cols(h)], qm[h])
            score[rows, :] = s
            return jnp.maximum(top, jnp.max(s.reshape(SEG // 8, 8, LANDMARKS), axis=0))

        top = lax.fori_loop(
            0, SEGS, far_scores, jnp.full((8, LANDMARKS), -jnp.inf, F32), unroll=True
        )
        top = jnp.max(top, axis=0, keepdims=True).astype(BF16).astype(F32)

        def far_weights(i, total):
            rows = pl.ds(pl.multiple_of(i * SEG, SEG), SEG)
            e = jnp.exp2((score[rows, :] - top) * SCALE2)
            wt[rows, :] = e.astype(BF16)
            return total + jnp.sum(e.reshape(SEG // 8, 8, LANDMARKS), axis=0)

        total = lax.fori_loop(
            0, SEGS, far_weights, jnp.zeros((8, LANDMARKS), F32), unroll=True
        )
        total = jnp.sum(total, axis=0, keepdims=True)
        total_hi = total.astype(BF16).astype(F32)
        total_lo = total - total_hi
        summed = dot(vt[h], wt[...])
        facts = jnp.zeros((SLICE, 128), F32)
        for n, (vec, half) in enumerate(
            (v, half) for v in (top, total_hi, total_lo) for half in range(2)
        ):
            part = jnp.broadcast_to(vec[:, half * 128 : (half + 1) * 128], (SLICE, 128))
            facts = jnp.where(row_id == n, part, facts)
        rs_send[h * OWN : (h + 1) * OWN, :, 0:LANDMARKS] = (
            summed.astype(BF16).reshape(OWN, SLICE, LANDMARKS)
        )
        rs_send[h * OWN : (h + 1) * OWN, :, LANDMARKS:PACK] = jnp.broadcast_to(
            facts.astype(BF16)[None], (OWN, SLICE, 128)
        )


    for h in range(HEADS):
        for n in range(1, OWN):
            j = (n + j_me) % OWN
            rs_copy(h * OWN + j, me, owner(h, j)).start()
    for n in range(1, HEADS):
        h = (h_me + n) % HEADS
        rs_copy(h * OWN + j_me, me, owner(h, j_me)).start()
    rs_total = rs_copy(pl.ds(0, SEQN - 1), pl.ds(0, SEQN - 1), other)
    rs_recv[me] = rs_send[h_me * OWN + j_me]

    down.wait_recv()
    up.wait_recv()
    v_pad[0:REACH, :] = jnp.where(me == 0, jnp.zeros((REACH, WIDTH), BF16), v_pad[0:REACH, :])
    v_pad[TOK + REACH : TOK + 2 * REACH, :] = jnp.where(
        me == SEQN - 1, jnp.zeros((REACH, WIDTH), BF16), v_pad[TOK + REACH : TOK + 2 * REACH, :]
    )
    conv_block(0)
    conv_block(TOK // 128 - 1)

    def near_softmax(i, _):
        rows = pl.ds(pl.multiple_of(i * SEG, SEG), SEG)
        for h in range(HEADS):
            s = dot(q_v[rows, cols(h)], kmt[h])
            e = jnp.exp2((s - jnp.max(s, axis=1, keepdims=True)) * SCALE2)
            near[h, rows, :] = (e * (1.0 / jnp.sum(e, axis=1, keepdims=True))).astype(BF16)
        return 0

    lax.fori_loop(0, NEAR_EARLY, near_softmax, 0)

    @pl.when(cme == 1)
    def _():
        top_total.wait_recv()
        top_over.start()

    @pl.when(cme == 0)
    def _():
        top_over.wait_recv()

    best = jnp.max(tops[...], axis=0)
    scale = 1.0 / (best[0:1, 0:1] * best[4:5, 0:1])
    m = mid[h_me]
    mb = m.astype(BF16)
    x_ref[0:LANDMARKS, :] = dot(m.T.astype(BF16), mb) * scale
    x_ref[LANDMARKS:, :] = m * scale

    def sweep(_, carry):
        x = x_ref[...]
        xb = x.astype(BF16)
        y = dot(xb, xb[:LANDMARKS])
        b = (7.0 * x[:LANDMARKS] - y[:LANDMARKS]).astype(BF16)
        x_ref[...] = 0.25 * (13.0 * x - 15.0 * y + dot(y.astype(BF16), b))
        return carry

    lax.fori_loop(0, SWEEPS, sweep, 0)

    rs_total.wait_recv()


    def facts_top(s, top):
        return jnp.maximum(top, rs_recv[s, :, LANDMARKS:PACK].astype(F32))

    top = lax.fori_loop(0, SEQN, facts_top, jnp.full((SLICE, 128), -jnp.inf, F32))

    def combine(s, carry):
        num, den = carry
        facts = rs_recv[s, :, LANDMARKS:PACK].astype(F32)
        e = jnp.exp2((facts - top) * SCALE2)
        w = jnp.concatenate([e[0:1], e[1:2]], axis=1)
        part = jnp.concatenate([facts[2:3] + facts[4:5], facts[3:4] + facts[5:6]], axis=1)
        return num + rs_recv[s, :, 0:LANDMARKS].astype(F32) * w, den + part * w

    num, den = lax.fori_loop(
        0, SEQN, combine, (jnp.zeros((SLICE, LANDMARKS), F32), jnp.zeros((1, LANDMARKS), F32))
    )
    reduced = (num / den).astype(BF16)
    slot = (h_me // 2) * OWN + j_me
    mp_all[cme, slot] = dot(reduced, x_ref[LANDMARKS:, :].astype(BF16)).astype(BF16)
    for r in range(1, CHIPS):
        group_copy(mp_all, (cme, slot), (mp_s, mp_r), 0, across(r)).start()
    mp_total = group_copy(mp_all, (0, pl.ds(0, CHIPS - 1)), (mp_s, mp_r), 0, other)
    mp_out = group_copy(mp_all, (cme,), (mp_s, mp_r), 1, other)
    mp_in = group_copy(mp_all, (1 - cme,), (mp_s, mp_r), 1, other)

    lax.fori_loop(NEAR_EARLY, SEGS, near_softmax, 0)

    mp_total.wait_recv()
    mp_out.start()

    def attend(h):
        lanes = pl.ds(pl.multiple_of(h * HEAD_DIM, HEAD_DIM), HEAD_DIM)
        mapped = mp_all[h % 2, pl.ds((h // 2) * OWN, OWN)].reshape(HEAD_DIM, LANDMARKS).astype(F32).T.astype(BF16)
        for i in range(4):
            rows = slice(i * 512, (i + 1) * 512)
            out[rows, lanes] = (dot(near[h, rows, :], mapped) + conv[rows, lanes]).astype(BF16)

    attend(cme)
    attend(cme + 2)

    mp_in.wait_recv()

    attend(1 - cme)
    attend(3 - cme)

    down.wait_send()
    up.wait_send()
    lm_total.wait_send()
    lm_out.wait_send()
    @pl.when(cme == 1)
    def _():
        top_total.wait_send()
        top_over.wait_send()

    rs_total.wait_send()
    mp_total.wait_send()
    mp_out.wait_send()


def shards(q, k, v, qs, ks, vs, cw):
    dma = pltpu.SemaphoreType.DMA
    vm = pltpu.VMEM
    hbm = pl.BlockSpec(memory_space=pl.ANY)
    whole = pl.BlockSpec(memory_space=pltpu.VMEM)
    taps = jnp.pad(cw, ((0, 0), (0, TOK - TAPS)))
    small = jnp.concatenate([qs.T, ks.T, vs.T, taps], axis=0)
    return pl.pallas_call(
        kernel,
        out_shape=jax.ShapeDtypeStruct((TOK, WIDTH), BF16),
        in_specs=[hbm, hbm, hbm, whole],
        out_specs=whole,
        scratch_shapes=[
            vm((TOK, WIDTH), BF16),
            vm((TOK, WIDTH), BF16),
            vm((TOK, WIDTH), BF16),
            vm((TOK + 128, WIDTH), BF16),
            vm((HEADS, HEAD_DIM, TOK), BF16),
            vm((TOK, 8), F32),
            vm((TOK, 8), F32),
            vm((2, CHIPS, 2 * SEGS, WIDTH), BF16),
            vm((HEADS, LANDMARKS, HEAD_DIM), BF16),
            vm((HEADS, LANDMARKS, HEAD_DIM), BF16),
            vm((HEADS, HEAD_DIM, LANDMARKS), BF16),
            vm((HEADS, LANDMARKS, LANDMARKS), F32),
            vm((HEADN, 8, 128), F32),
            vm((TOK, LANDMARKS), F32),
            vm((TOK, LANDMARKS), BF16),
            vm((SEQN, SLICE, PACK), BF16),
            vm((SEQN, SLICE, PACK), BF16),
            vm((2 * LANDMARKS, LANDMARKS), F32),
            vm((HEADS, TOK, LANDMARKS), BF16),
            vm((TOK, WIDTH), F32),
            vm((2, CHIPS, SLICE, LANDMARKS), BF16),
            vm((HEADS, 128, 256), BF16),
            dma((SEGS,)),
            dma((SEGS,)),
            dma((SEGS,)),
            dma((2,)),
            dma((2,)),
            dma((2,)),
            dma((2,)),
            dma((2,)),
            dma((2,)),
            dma((1,)),
            dma((1,)),
            dma((2,)),
            dma((2,)),
            pltpu.SemaphoreType.REGULAR,
        ],
        compiler_params=pltpu.CompilerParams(
            collective_id=0, has_side_effects=True, vmem_limit_bytes=50 * 1024 * 1024
        ),
        name="nystrom",
    )(q, k, v, small)


def solution(mesh):
    tokens, heads = P("seq", "head"), P("head", None)
    return jax.shard_map(
        shards, mesh=mesh, in_specs=(tokens,) * 6 + (heads,), out_specs=tokens, check_vma=False
    )
```

```python
import functools
import math

import jax
import jax.numpy as jnp
from jax import lax
from jax.experimental import pallas as pl
from jax.experimental.pallas import tpu as pltpu
from jax.sharding import PartitionSpec as P

MESH = pl.DeviceIdType.MESH
F32 = jnp.float32
BF16 = jnp.bfloat16
HEAD_DIM = 128
LANDMARKS = 256
SWEEPS = 6
TAPS = 33
REACH = TAPS // 2
LOG2E = math.log2(math.e)
SCALE2 = HEAD_DIM**-0.5 * LOG2E
FACTOR = HEAD_DIM**-0.5

TOK = 2048
HEADS = 4
WIDTH = HEADS * HEAD_DIM
SEQN = 32
HEADN = 8
SEGS = 8
SEG = 256
CHIPS = SEQN // 2
OWN = 8
SLICE = HEAD_DIM // OWN
NEAR_EARLY = 4
KEYS_EARLY = 2


def dot(a, b):
    return jnp.dot(a, b, preferred_element_type=F32)


def dot_nt(a, b):
    return lax.dot_general(a, b, (((1,), (1,)), ((), ())), preferred_element_type=F32)


def cols(h):
    return slice(h * HEAD_DIM, (h + 1) * HEAD_DIM)


def kernel(
    q_hbm, k_hbm, v_hbm, small, out,
    q_v, k_v, v_raw, v_pad, vt, sc_qk, sc_v, lm_all, qm, kmt,
    mid, tops, score, wt, rs_send, rs_recv, fact_send, fact_recv, x_ref, near, conv, mp_all, toep,
    q_sem, k_sem, v_sem, lm_s, lm_r, halo_s, halo_r, top_s, top_r, rs_s, rs_r, mp_s, mp_r, go_sem,
):
    me = lax.axis_index("seq")
    zme = lax.axis_index("head")
    yme, xme, cme = me // 8, (me // 2) % 4, me % 2
    h_me = 2 * ((xme + yme) % 2) + cme
    j_me = (me // 2) // 2
    chip = me // 2
    other = me + 1 - 2 * cme

    def partner(r):
        return (
            ((yme + r // 8) % 4) * 8 + ((xme + (r // 2) % 4) % 4) * 2 + (cme + r % 2) % 2
        )

    def across(r):
        return ((yme + r // 4) % 4) * 8 + ((xme + r % 4) % 4) * 2 + cme

    def owner(h, j):
        y = j // 2
        return (4 * y + 2 * (j % 2) + (h // 2 + y) % 2) * 2 + h % 2

    def rows_copy(src, dst, sem, i):
        rows = pl.ds(i * SEG, SEG)
        return pltpu.make_async_copy(src.at[rows], dst.at[rows], sem.at[i])

    barrier = pltpu.get_barrier_semaphore()

    def greet(r, _):
        target = ((yme + r // 4) % 4) * 8 + ((xme + r % 4) % 4) * 2
        pl.semaphore_signal(barrier, inc=1, device_id=(target, zme), device_id_type=MESH)
        return 0

    lax.fori_loop(1, CHIPS, greet, 0)

    @pl.when(cme == 1)
    def _():
        pl.semaphore_signal(barrier, inc=1, device_id=(other, zme), device_id_type=MESH)

    for i in range(SEGS):
        rows_copy(q_hbm, q_v, q_sem, i).start()
    for i in range(SEGS):
        rows_copy(k_hbm, k_v, k_sem, i).start()
    for i in range(SEGS):
        rows_copy(v_hbm, v_raw, v_sem, i).start()

    sc_qk[...] = small[0 : 2 * HEADS, :].T
    sc_v[...] = small[2 * HEADS : 4 * HEADS, :].T

    seg_id = lax.broadcasted_iota(jnp.int32, (SEGS, HEAD_DIM), 0)

    no_marks = (jnp.zeros((SEGS, HEAD_DIM), F32),) * HEADS

    def scale_means(t, src, buf, sem, first, end, marks):
        def segment(i, marks):
            rows = pl.ds(pl.multiple_of(i * SEG, SEG), SEG)
            rows_copy(src, buf, sem, i).wait()
            following = []
            for h in range(HEADS):
                n = t * HEADS + h
                x = (buf[rows, cols(h)].astype(F32) * sc_qk[rows, n : n + 1]).astype(BF16)
                buf[rows, cols(h)] = x
                mean = jnp.sum(x.astype(F32), axis=0, keepdims=True) * (1.0 / SEG)
                following.append(jnp.where(seg_id == i, mean, marks[h]))
            return tuple(following)

        return lax.fori_loop(first, end, segment, marks)

    def own_marks(t, marks):
        for n in range(2):
            both = jnp.concatenate([marks[n], marks[n + 2]], axis=0)
            lm_all[t, cme, chip, :, cols(n)] = both.astype(BF16)

    own_marks(0, scale_means(0, q_hbm, q_v, q_sem, 0, SEGS, no_marks))
    key_marks = scale_means(1, k_hbm, k_v, k_sem, 0, KEYS_EARLY, no_marks)

    @pl.when(cme == 0)
    def _():
        pl.semaphore_wait(barrier, SEQN - 1)
        pl.semaphore_signal(go_sem, inc=1, device_id=(other, zme), device_id_type=MESH)

    @pl.when(cme == 1)
    def _():
        pl.semaphore_wait(go_sem, 1)
        for r in range(1, HEADN):
            pl.semaphore_signal(
                barrier, inc=1, device_id=(me, (zme + r) % HEADN), device_id_type=MESH
            )

    def group_copy(buf, at, sems, n, target):
        return pltpu.make_async_remote_copy(
            src_ref=buf.at[at],
            dst_ref=buf.at[at],
            send_sem=sems[0].at[n],
            recv_sem=sems[1].at[n],
            device_id=(target, zme),
            device_id_type=MESH,
        )

    def leave(t):
        for r in range(1, CHIPS):
            group_copy(lm_all, (t, cme, chip), (lm_s, lm_r), t, across(r)).start()

    lm_total = [
        group_copy(lm_all, (t, 0, pl.ds(0, CHIPS - 1)), (lm_s, lm_r), t, other) for t in range(2)
    ]
    lm_out = [group_copy(lm_all, (t, cme), (lm_s, lm_r), 2 + t, other) for t in range(2)]
    lm_in = [group_copy(lm_all, (t, 1 - cme), (lm_s, lm_r), 2 + t, other) for t in range(2)]
    leave(0)

    own_marks(1, scale_means(1, k_hbm, k_v, k_sem, KEYS_EARLY, SEGS, key_marks))
    leave(1)

    def scale_v(i, _):
        rows = pl.ds(pl.multiple_of(i * SEG, SEG), SEG)
        out_rows = pl.ds(pl.multiple_of(i * SEG + REACH, REACH), SEG)
        rows_copy(v_hbm, v_raw, v_sem, i).wait()
        for h in range(HEADS):
            x = (v_raw[rows, cols(h)].astype(F32) * sc_v[rows, h : h + 1]).astype(BF16)
            v_pad[out_rows, cols(h)] = x
            vt[h, :, rows] = x.astype(F32).T.astype(BF16)
        return 0

    lax.fori_loop(0, SEGS, scale_v, 0, unroll=2)
    v_pad[TOK + 2 * REACH :, :] = jnp.zeros((128 - 2 * REACH, WIDTH), BF16)

    after, before = (me + 1) % SEQN, (me + SEQN - 1) % SEQN
    down = pltpu.make_async_remote_copy(
        src_ref=v_pad.at[pl.ds(TOK, REACH)],
        dst_ref=v_pad.at[pl.ds(0, REACH)],
        send_sem=halo_s.at[0],
        recv_sem=halo_r.at[0],
        device_id=(after, zme),
        device_id_type=MESH,
    )
    up = pltpu.make_async_remote_copy(
        src_ref=v_pad.at[pl.ds(REACH, REACH)],
        dst_ref=v_pad.at[pl.ds(TOK + REACH, REACH)],
        send_sem=halo_s.at[1],
        recv_sem=halo_r.at[1],
        device_id=(before, zme),
        device_id_type=MESH,
    )
    down.start()
    up.start()

    for h in range(HEADS):
        line = jnp.broadcast_to(small[3 * HEADS + h : 3 * HEADS + h + 1, 0:256], (128, 256))
        toep[h] = pltpu.roll(line, 0, 1, stride=1, stride_axis=0).astype(BF16)

    def conv_block(b):
        window = pl.ds(pl.multiple_of(b * 128, 128), 256)
        rows = pl.ds(pl.multiple_of(b * 128, 128), 128)
        for h in range(HEADS):
            conv[rows, cols(h)] = dot(toep[h], v_pad[window, cols(h)])

    def conv_inner(b, _):
        conv_block(b)
        return 0

    lm_total[0].wait_recv()
    lm_out[0].start()

    lax.fori_loop(1, TOK // 128 - 1, conv_inner, 0, unroll=True)

    lm_total[1].wait_recv()
    lm_out[1].start()

    lm_in[0].wait_recv()

    def by_head(t, h):
        both = lm_all[t, :, :, :, cols(h % 2)].reshape(SEQN, 2 * SEGS, HEAD_DIM).astype(F32)
        at = (h // 2) * SEGS
        return both[:, at : at + SEGS].reshape(LANDMARKS, HEAD_DIM)

    for h in range(HEADS):
        qm[h] = by_head(0, h).astype(BF16)

    def rs_copy(bufs, n, block, slot, target):
        return pltpu.make_async_remote_copy(
            src_ref=bufs[0].at[block],
            dst_ref=bufs[1].at[slot],
            send_sem=rs_s.at[n],
            recv_sem=rs_r.at[n],
            device_id=(target, zme),
            device_id_type=MESH,
        )

    sums, facts = (rs_send, rs_recv), (fact_send, fact_recv)
    tops_of, totals_of = {}, {}

    def far_scores(h):
        def chunk(i, top):
            rows = pl.ds(pl.multiple_of(i * SEG, SEG), SEG)
            s = dot_nt(k_v[rows, cols(h)], qm[h])
            score[h % 2, rows, :] = s
            return jnp.maximum(top, jnp.max(s.reshape(SEG // 8, 8, LANDMARKS), axis=0))

        top = lax.fori_loop(
            0, SEGS, chunk, jnp.full((8, LANDMARKS), -jnp.inf, F32), unroll=True
        )
        tops_of[h] = jnp.max(top, axis=0, keepdims=True)

    def far_weights(h):
        top = tops_of[h]

        def chunk(i, total):
            rows = pl.ds(pl.multiple_of(i * SEG, SEG), SEG)
            e = jnp.exp2((score[h % 2, rows, :] - top) * SCALE2)
            wt[h % 2, rows, :] = e.astype(BF16)
            return total + jnp.sum(e.reshape(SEG // 8, 8, LANDMARKS), axis=0)

        total = lax.fori_loop(0, SEGS, chunk, jnp.zeros((8, LANDMARKS), F32), unroll=True)
        totals_of[h] = jnp.sum(total, axis=0, keepdims=True)

    def far_sums(h):
        summed = dot(vt[h], wt[h % 2])
        rs_send[h * OWN : (h + 1) * OWN] = summed.astype(BF16).reshape(OWN, SLICE, LANDMARKS)
        top, total = tops_of[h], totals_of[h]
        lines = jnp.concatenate(
            [top[:, :128], top[:, 128:], total[:, :128], total[:, 128:]], axis=0
        )
        fact_send[h * OWN : (h + 1) * OWN] = jnp.broadcast_to(lines[None], (OWN, 4, 128))

    def far_leave(h):
        for n in range(1, OWN):
            j = (n + j_me) % OWN
            target = owner(h, j)
            rs_copy(sums, 0, h * OWN + j, me, target).start()
            rs_copy(facts, 1, h * OWN + j, me, target).start()

    far_scores(0)
    far_scores(1)

    lm_in[1].wait_recv()
    for h in range(HEADS):
        kmt[h] = by_head(1, h).T.astype(BF16)

    col_top = jnp.zeros((1, 1), F32)
    row_top = jnp.zeros((1, 1), F32)
    for h in range(HEADS):
        s = dot(qm[h], kmt[h])
        e = jnp.exp2((s - jnp.max(s, axis=1, keepdims=True)) * SCALE2)
        m = e / jnp.sum(e, axis=1, keepdims=True)
        mid[h] = m
        c = jnp.sum(m, axis=0, keepdims=True)
        r = jnp.sum(m, axis=1, keepdims=True)
        col_top = jnp.maximum(col_top, jnp.max(c, axis=1, keepdims=True))
        row_top = jnp.maximum(row_top, jnp.max(r, axis=0, keepdims=True))
    first_half = lax.broadcasted_iota(jnp.int32, (8, 128), 0) < 4
    own_top = jnp.where(
        first_half, jnp.broadcast_to(col_top, (8, 128)), jnp.broadcast_to(row_top, (8, 128))
    )

    tops[zme] = own_top

    def top_copy(at, core, target):
        return pltpu.make_async_remote_copy(
            src_ref=tops.at[at],
            dst_ref=tops.at[at],
            send_sem=top_s.at[core],
            recv_sem=top_r.at[0],
            device_id=(2 * chip + core, target),
            device_id_type=MESH,
        )

    @pl.when(cme == 1)
    def _():
        pl.semaphore_wait(barrier, HEADN - 1)
        for r in range(1, HEADN):
            top_copy(zme, 0, (zme + r) % HEADN).start()
            top_copy(zme, 1, (zme + r) % HEADN).start()

    top_total = [top_copy(pl.ds(0, HEADN - 1), core, zme) for core in range(2)]

    far_weights(0)
    far_sums(0)
    far_scores(2)
    far_weights(1)
    far_leave(0)
    far_sums(1)
    far_scores(3)
    far_weights(2)
    far_leave(1)
    far_sums(2)
    far_weights(3)
    far_leave(2)
    far_sums(3)
    far_leave(3)
    for n in range(1, HEADS):
        h = (h_me + n) % HEADS
        rs_copy(sums, 0, h * OWN + j_me, me, owner(h, j_me)).start()
        rs_copy(facts, 1, h * OWN + j_me, me, owner(h, j_me)).start()
    rs_total = [
        rs_copy(bufs, n, pl.ds(0, SEQN - 1), pl.ds(0, SEQN - 1), other)
        for n, bufs in enumerate((sums, facts))
    ]
    rs_recv[me] = rs_send[h_me * OWN + j_me]
    fact_recv[me] = fact_send[h_me * OWN + j_me]

    down.wait_recv()
    up.wait_recv()
    v_pad[0:REACH, :] = jnp.where(me == 0, jnp.zeros((REACH, WIDTH), BF16), v_pad[0:REACH, :])
    v_pad[TOK + REACH : TOK + 2 * REACH, :] = jnp.where(
        me == SEQN - 1, jnp.zeros((REACH, WIDTH), BF16), v_pad[TOK + REACH : TOK + 2 * REACH, :]
    )
    conv_block(0)
    conv_block(TOK // 128 - 1)

    def near_softmax(i, _):
        rows = pl.ds(pl.multiple_of(i * SEG, SEG), SEG)
        for h in range(HEADS):
            s = dot(q_v[rows, cols(h)], kmt[h])
            e = jnp.exp2((s - jnp.max(s, axis=1, keepdims=True)) * SCALE2)
            near[h, rows, :] = (e * (1.0 / jnp.sum(e, axis=1, keepdims=True))).astype(BF16)
        return 0

    lax.fori_loop(0, NEAR_EARLY, near_softmax, 0)

    m = mid[h_me]
    mb = m.astype(BF16)
    x_ref[0:LANDMARKS, :] = dot(m.T.astype(BF16), mb)
    x_ref[LANDMARKS:, :] = m
    top_total[0].wait_recv()

    best = jnp.max(tops[...], axis=0)
    scale = 1.0 / (best[0:1, 0:1] * best[4:5, 0:1])
    x = x_ref[...] * scale
    for sweep in range(SWEEPS):
        xb = x.astype(BF16)
        y = dot(xb, xb[:LANDMARKS])
        b = (7.0 * x[:LANDMARKS] - y[:LANDMARKS]).astype(BF16)
        if sweep == SWEEPS - 1:
            x, y = x[LANDMARKS:], y[LANDMARKS:]
        x = 0.25 * (13.0 * x - 15.0 * y + dot(y.astype(BF16), b))
    iterated = x.astype(BF16)

    for copy in rs_total:
        copy.wait_recv()


    top = jnp.max(fact_recv[...], axis=0)

    def combine(s, carry):
        num, den = carry
        lines = fact_recv[s]
        e = jnp.exp2((lines - top) * SCALE2)
        w = jnp.concatenate([e[0:1], e[1:2]], axis=1)
        part = jnp.concatenate([lines[2:3], lines[3:4]], axis=1)
        return num + rs_recv[s].astype(F32) * w, den + part * w

    num, den = lax.fori_loop(
        0,
        SEQN,
        combine,
        (jnp.zeros((SLICE, LANDMARKS), F32), jnp.zeros((1, LANDMARKS), F32)),
        unroll=4,
    )
    reduced = (num / den).astype(BF16)
    slot = (h_me // 2) * OWN + j_me
    mp_all[cme, slot] = dot(reduced, iterated).astype(BF16)
    for r in range(1, CHIPS):
        group_copy(mp_all, (cme, slot), (mp_s, mp_r), 0, across(r)).start()
    mp_total = group_copy(mp_all, (0, pl.ds(0, CHIPS - 1)), (mp_s, mp_r), 0, other)
    mp_out = group_copy(mp_all, (cme,), (mp_s, mp_r), 1, other)
    mp_in = group_copy(mp_all, (1 - cme,), (mp_s, mp_r), 1, other)

    lax.fori_loop(NEAR_EARLY, SEGS, near_softmax, 0)

    mp_total.wait_recv()
    mp_out.start()

    def attend(h):
        lanes = pl.ds(pl.multiple_of(h * HEAD_DIM, HEAD_DIM), HEAD_DIM)
        mapped = mp_all[h % 2, pl.ds((h // 2) * OWN, OWN)].reshape(HEAD_DIM, LANDMARKS).astype(F32).T.astype(BF16)
        for i in range(4):
            rows = slice(i * 512, (i + 1) * 512)
            out[rows, lanes] = (dot(near[h, rows, :], mapped) + conv[rows, lanes]).astype(BF16)

    attend(cme)
    attend(cme + 2)

    mp_in.wait_recv()

    attend(1 - cme)
    attend(3 - cme)

    down.wait_send()
    up.wait_send()
    for copy in lm_total + lm_out:
        copy.wait_send()
    @pl.when(cme == 1)
    def _():
        for copy in top_total:
            copy.wait_send()

    for copy in rs_total:
        copy.wait_send()
    mp_total.wait_send()
    mp_out.wait_send()


def shards(q, k, v, qs, ks, vs, cw):
    dma = pltpu.SemaphoreType.DMA
    vm = pltpu.VMEM
    hbm = pl.BlockSpec(memory_space=pl.ANY)
    whole = pl.BlockSpec(memory_space=pltpu.VMEM)
    taps = jnp.pad(cw, ((0, 0), (0, TOK - TAPS)))
    small = jnp.concatenate([qs.T, ks.T, vs.T, taps], axis=0)
    return pl.pallas_call(
        kernel,
        out_shape=jax.ShapeDtypeStruct((TOK, WIDTH), BF16),
        in_specs=[hbm, hbm, hbm, whole],
        out_specs=whole,
        scratch_shapes=[
            vm((TOK, WIDTH), BF16),
            vm((TOK, WIDTH), BF16),
            vm((TOK, WIDTH), BF16),
            vm((TOK + 128, WIDTH), BF16),
            vm((HEADS, HEAD_DIM, TOK), BF16),
            vm((TOK, 8), F32),
            vm((TOK, 8), F32),
            vm((2, 2, CHIPS, 2 * SEGS, WIDTH // 2), BF16),
            vm((HEADS, LANDMARKS, HEAD_DIM), BF16),
            vm((HEADS, HEAD_DIM, LANDMARKS), BF16),
            vm((HEADS, LANDMARKS, LANDMARKS), F32),
            vm((HEADN, 8, 128), F32),
            vm((2, TOK, LANDMARKS), F32),
            vm((2, TOK, LANDMARKS), BF16),
            vm((SEQN, SLICE, LANDMARKS), BF16),
            vm((SEQN, SLICE, LANDMARKS), BF16),
            vm((SEQN, 4, 128), F32),
            vm((SEQN, 4, 128), F32),
            vm((2 * LANDMARKS, LANDMARKS), F32),
            vm((HEADS, TOK, LANDMARKS), BF16),
            vm((TOK, WIDTH), F32),
            vm((2, CHIPS, SLICE, LANDMARKS), BF16),
            vm((HEADS, 128, 256), BF16),
            dma((SEGS,)),
            dma((SEGS,)),
            dma((SEGS,)),
            dma((4,)),
            dma((4,)),
            dma((2,)),
            dma((2,)),
            dma((2,)),
            dma((2,)),
            dma((2,)),
            dma((2,)),
            dma((2,)),
            dma((2,)),
            pltpu.SemaphoreType.REGULAR,
        ],
        compiler_params=pltpu.CompilerParams(
            collective_id=0, has_side_effects=True, vmem_limit_bytes=50 * 1024 * 1024
        ),
        name="nystrom",
    )(q, k, v, small)


def solution(mesh):
    tokens, heads = P("seq", "head"), P("head", None)
    return jax.shard_map(
        shards, mesh=mesh, in_specs=(tokens,) * 6 + (heads,), out_specs=tokens, check_vma=False
    )
```

```python
import functools
import math

import jax
import jax.numpy as jnp
from jax import lax
from jax.experimental import pallas as pl
from jax.experimental.pallas import tpu as pltpu
from jax.sharding import PartitionSpec as P

MESH = pl.DeviceIdType.MESH
F32 = jnp.float32
BF16 = jnp.bfloat16
HEAD_DIM = 128
LANDMARKS = 256
SWEEPS = 6
TAPS = 33
REACH = TAPS // 2
LOG2E = math.log2(math.e)
SCALE2 = HEAD_DIM**-0.5 * LOG2E
FACTOR = HEAD_DIM**-0.5

TOK = 2048
HEADS = 4
WIDTH = HEADS * HEAD_DIM
SEQN = 32
HEADN = 8
SEGS = 8
SEG = 256
CHIPS = SEQN // 2
OWN = 8
SLICE = HEAD_DIM // OWN
KEYS_EARLY = 3


def dot(a, b):
    return jnp.dot(a, b, preferred_element_type=F32)


def dot_nt(a, b):
    return lax.dot_general(a, b, (((1,), (1,)), ((), ())), preferred_element_type=F32)


def cols(h):
    return slice(h * HEAD_DIM, (h + 1) * HEAD_DIM)


def kernel(
    q_hbm, k_hbm, v_hbm, small, out,
    q_v, k_v, v_raw, v_pad, vt, sc_qk, sc_v, lm_all, qm, kmt,
    mid, tops, score, wt, rs_send, rs_recv, fact_send, fact_recv, x_ref, near, conv, rd_all, mp_all, toep,
    q_sem, k_sem, v_sem, lm_s, lm_r, halo_s, halo_r, top_s, top_r, rs_s, rs_r, mp_s, mp_r, go_sem,
):
    me = lax.axis_index("seq")
    zme = lax.axis_index("head")
    yme, xme, cme = me // 8, (me // 2) % 4, me % 2
    h_me = 2 * ((xme + yme) % 2) + cme
    j_me = (me // 2) // 2
    chip = me // 2
    other = me + 1 - 2 * cme

    def partner(r):
        return (
            ((yme + r // 8) % 4) * 8 + ((xme + (r // 2) % 4) % 4) * 2 + (cme + r % 2) % 2
        )

    def across(r):
        return ((yme + r // 4) % 4) * 8 + ((xme + r % 4) % 4) * 2 + cme

    def owner(h, j):
        y = j // 2
        return (4 * y + 2 * (j % 2) + (h // 2 + y) % 2) * 2 + h % 2

    def rows_copy(src, dst, sem, i):
        rows = pl.ds(i * SEG, SEG)
        return pltpu.make_async_copy(src.at[rows], dst.at[rows], sem.at[i])

    for i in range(SEGS):
        rows_copy(q_hbm, q_v, q_sem, i).start()
    for i in range(SEGS):
        rows_copy(k_hbm, k_v, k_sem, i).start()
    for i in range(SEGS):
        rows_copy(v_hbm, v_raw, v_sem, i).start()

    barrier = pltpu.get_barrier_semaphore()

    for r in range(1, CHIPS):
        target = ((yme + r // 4) % 4) * 8 + ((xme + r % 4) % 4) * 2
        pl.semaphore_signal(barrier, inc=1, device_id=(target, zme), device_id_type=MESH)

    @pl.when(cme == 1)
    def _():
        pl.semaphore_signal(barrier, inc=1, device_id=(other, zme), device_id_type=MESH)

    sc_qk[...] = small[0 : 2 * HEADS, :].T

    seg_id = lax.broadcasted_iota(jnp.int32, (SEGS, HEAD_DIM), 0)

    no_marks = (jnp.zeros((SEGS, HEAD_DIM), F32),) * HEADS

    def scale_means(t, src, buf, sem, first, end, marks):
        def segment(i, marks):
            rows = pl.ds(pl.multiple_of(i * SEG, SEG), SEG)
            rows_copy(src, buf, sem, i).wait()
            following = []
            for h in range(HEADS):
                n = t * HEADS + h
                x = (buf[rows, cols(h)].astype(F32) * sc_qk[rows, n : n + 1]).astype(BF16)
                buf[rows, cols(h)] = x
                mean = jnp.sum(x.astype(F32), axis=0, keepdims=True) * (1.0 / SEG)
                following.append(jnp.where(seg_id == i, mean, marks[h]))
            return tuple(following)

        return lax.fori_loop(first, end, segment, marks)

    def own_marks(t, marks):
        for n in range(2):
            both = jnp.concatenate([marks[n], marks[n + 2]], axis=0)
            lm_all[t, cme, chip, :, cols(n)] = both.astype(BF16)

    own_marks(0, scale_means(0, q_hbm, q_v, q_sem, 0, SEGS, no_marks))
    key_marks = scale_means(1, k_hbm, k_v, k_sem, 0, KEYS_EARLY, no_marks)

    @pl.when(cme == 0)
    def _():
        pl.semaphore_wait(barrier, SEQN - 1)
        pl.semaphore_signal(go_sem, inc=1, device_id=(other, zme), device_id_type=MESH)

    @pl.when(cme == 1)
    def _():
        pl.semaphore_wait(go_sem, 1)
        for r in range(1, HEADN):
            pl.semaphore_signal(
                barrier, inc=1, device_id=(me, (zme + r) % HEADN), device_id_type=MESH
            )

    def group_copy(buf, at, sems, n, target):
        return pltpu.make_async_remote_copy(
            src_ref=buf.at[at],
            dst_ref=buf.at[at],
            send_sem=sems[0].at[n],
            recv_sem=sems[1].at[n],
            device_id=(target, zme),
            device_id_type=MESH,
        )

    def leave(t):
        for r in range(1, CHIPS):
            group_copy(lm_all, (t, cme, chip), (lm_s, lm_r), t, across(r)).start()

    lm_total = [
        group_copy(lm_all, (t, 0, pl.ds(0, CHIPS - 1)), (lm_s, lm_r), t, other) for t in range(2)
    ]
    lm_out = [group_copy(lm_all, (t, cme), (lm_s, lm_r), 2 + t, other) for t in range(2)]
    lm_in = [group_copy(lm_all, (t, 1 - cme), (lm_s, lm_r), 2 + t, other) for t in range(2)]
    leave(0)

    own_marks(1, scale_means(1, k_hbm, k_v, k_sem, KEYS_EARLY, SEGS, key_marks))
    leave(1)

    sc_v[...] = small[2 * HEADS : 4 * HEADS, :].T
    def scale_v(i, _):
        rows = pl.ds(pl.multiple_of(i * SEG, SEG), SEG)
        out_rows = pl.ds(pl.multiple_of(i * SEG + REACH, REACH), SEG)
        rows_copy(v_hbm, v_raw, v_sem, i).wait()
        for h in range(HEADS):
            x = (v_raw[rows, cols(h)].astype(F32) * sc_v[rows, h : h + 1]).astype(BF16)
            v_pad[out_rows, cols(h)] = x
            vt[h, :, rows] = x.astype(F32).T.astype(BF16)
        return 0

    lax.fori_loop(0, SEGS, scale_v, 0, unroll=2)
    v_pad[TOK + 2 * REACH :, :] = jnp.zeros((128 - 2 * REACH, WIDTH), BF16)

    after, before = (me + 1) % SEQN, (me + SEQN - 1) % SEQN
    down = pltpu.make_async_remote_copy(
        src_ref=v_pad.at[pl.ds(TOK, REACH)],
        dst_ref=v_pad.at[pl.ds(0, REACH)],
        send_sem=halo_s.at[0],
        recv_sem=halo_r.at[0],
        device_id=(after, zme),
        device_id_type=MESH,
    )
    up = pltpu.make_async_remote_copy(
        src_ref=v_pad.at[pl.ds(REACH, REACH)],
        dst_ref=v_pad.at[pl.ds(TOK + REACH, REACH)],
        send_sem=halo_s.at[1],
        recv_sem=halo_r.at[1],
        device_id=(before, zme),
        device_id_type=MESH,
    )
    down.start()
    up.start()

    for h in range(HEADS):
        line = jnp.broadcast_to(small[3 * HEADS + h : 3 * HEADS + h + 1, 0:256], (128, 256))
        toep[h] = pltpu.roll(line, 0, 1, stride=1, stride_axis=0).astype(BF16)

    def conv_block(b):
        window = pl.ds(pl.multiple_of(b * 128, 128), 256)
        rows = pl.ds(pl.multiple_of(b * 128, 128), 128)
        for h in range(HEADS):
            conv[rows, cols(h)] = dot(toep[h], v_pad[window, cols(h)])

    def conv_inner(b, _):
        conv_block(b)
        return 0

    lm_total[0].wait_recv()
    lm_out[0].start()

    lax.fori_loop(1, TOK // 128 - 1, conv_inner, 0, unroll=True)

    lm_total[1].wait_recv()
    lm_out[1].start()

    lm_in[0].wait_recv()

    def by_head(t, h):
        both = lm_all[t, :, :, :, cols(h % 2)].reshape(SEQN, 2 * SEGS, HEAD_DIM).astype(F32)
        at = (h // 2) * SEGS
        return both[:, at : at + SEGS].reshape(LANDMARKS, HEAD_DIM)

    for h in range(HEADS):
        qm[h] = by_head(0, h).astype(BF16)

    def rs_copy(bufs, n, block, slot, target):
        return pltpu.make_async_remote_copy(
            src_ref=bufs[0].at[block],
            dst_ref=bufs[1].at[slot],
            send_sem=rs_s.at[n],
            recv_sem=rs_r.at[n],
            device_id=(target, zme),
            device_id_type=MESH,
        )

    sums, facts = (rs_send, rs_recv), (fact_send, fact_recv)
    tops_of, totals_of = {}, {}

    def far_scores(h):
        def chunk(i, top):
            rows = pl.ds(pl.multiple_of(i * SEG, SEG), SEG)
            s = dot_nt(k_v[rows, cols(h)], qm[h])
            score[h % 2, rows, :] = s
            return jnp.maximum(top, jnp.max(s.reshape(SEG // 8, 8, LANDMARKS), axis=0))

        top = lax.fori_loop(
            0, SEGS, chunk, jnp.full((8, LANDMARKS), -jnp.inf, F32), unroll=True
        )
        tops_of[h] = jnp.max(top, axis=0, keepdims=True)

    def far_weights(h):
        top = tops_of[h]

        def chunk(i, total):
            rows = pl.ds(pl.multiple_of(i * SEG, SEG), SEG)
            e = jnp.exp2((score[h % 2, rows, :] - top) * SCALE2)
            wt[h % 2, rows, :] = e.astype(BF16)
            return total + jnp.sum(e.reshape(SEG // 8, 8, LANDMARKS), axis=0)

        total = lax.fori_loop(0, SEGS, chunk, jnp.zeros((8, LANDMARKS), F32), unroll=True)
        totals_of[h] = jnp.sum(total, axis=0, keepdims=True)

    def far_sums(h):
        summed = dot(vt[h], wt[h % 2])
        rs_send[h * OWN : (h + 1) * OWN] = summed.astype(BF16).reshape(OWN, SLICE, LANDMARKS)
        top, total = tops_of[h], totals_of[h]
        lines = jnp.concatenate(
            [top[:, :128], top[:, 128:], total[:, :128], total[:, 128:]], axis=0
        )
        fact_send[h * OWN : (h + 1) * OWN] = jnp.broadcast_to(lines[None], (OWN, 4, 128))

    def far_leave(h):
        for n in range(1, OWN):
            j = (n + j_me) % OWN
            target = owner(h, j)
            rs_copy(sums, 0, h * OWN + j, me, target).start()
            rs_copy(facts, 1, h * OWN + j, me, target).start()

    far_scores(0)
    far_scores(1)

    lm_in[1].wait_recv()
    for h in range(HEADS):
        kmt[h] = by_head(1, h).T.astype(BF16)

    col_top = jnp.zeros((1, 1), F32)
    row_top = jnp.zeros((1, 1), F32)
    for h in range(HEADS):
        s = dot(qm[h], kmt[h])
        e = jnp.exp2((s - jnp.max(s, axis=1, keepdims=True)) * SCALE2)
        m = e / jnp.sum(e, axis=1, keepdims=True)
        mid[h] = m
        c = jnp.sum(m, axis=0, keepdims=True)
        r = jnp.sum(m, axis=1, keepdims=True)
        col_top = jnp.maximum(col_top, jnp.max(c, axis=1, keepdims=True))
        row_top = jnp.maximum(row_top, jnp.max(r, axis=0, keepdims=True))
    first_half = lax.broadcasted_iota(jnp.int32, (8, 128), 0) < 4
    own_top = jnp.where(
        first_half, jnp.broadcast_to(col_top, (8, 128)), jnp.broadcast_to(row_top, (8, 128))
    )

    tops[zme] = own_top

    def top_copy(at, core, target):
        return pltpu.make_async_remote_copy(
            src_ref=tops.at[at],
            dst_ref=tops.at[at],
            send_sem=top_s.at[core],
            recv_sem=top_r.at[0],
            device_id=(2 * chip + core, target),
            device_id_type=MESH,
        )

    @pl.when(cme == 1)
    def _():
        pl.semaphore_wait(barrier, HEADN - 1)
        for r in range(1, HEADN):
            top_copy(zme, 0, (zme + r) % HEADN).start()
            top_copy(zme, 1, (zme + r) % HEADN).start()

    top_total = [top_copy(pl.ds(0, HEADN - 1), core, zme) for core in range(2)]

    far_weights(0)
    far_sums(0)
    far_scores(2)
    far_weights(1)
    far_leave(0)
    far_sums(1)
    far_scores(3)
    far_weights(2)
    far_leave(1)
    far_sums(2)
    far_weights(3)
    far_leave(2)
    far_sums(3)
    far_leave(3)
    for n in range(1, HEADS):
        h = (h_me + n) % HEADS
        rs_copy(sums, 0, h * OWN + j_me, me, owner(h, j_me)).start()
        rs_copy(facts, 1, h * OWN + j_me, me, owner(h, j_me)).start()
    rs_total = [
        rs_copy(bufs, n, pl.ds(0, SEQN - 1), pl.ds(0, SEQN - 1), other)
        for n, bufs in enumerate((sums, facts))
    ]
    rs_recv[me] = rs_send[h_me * OWN + j_me]
    fact_recv[me] = fact_send[h_me * OWN + j_me]

    down.wait_recv()
    up.wait_recv()
    v_pad[0:REACH, :] = jnp.where(me == 0, jnp.zeros((REACH, WIDTH), BF16), v_pad[0:REACH, :])
    v_pad[TOK + REACH : TOK + 2 * REACH, :] = jnp.where(
        me == SEQN - 1, jnp.zeros((REACH, WIDTH), BF16), v_pad[TOK + REACH : TOK + 2 * REACH, :]
    )
    conv_block(0)
    conv_block(TOK // 128 - 1)

    def near_softmax(i, _):
        rows = pl.ds(pl.multiple_of(i * SEG, SEG), SEG)
        for h in range(HEADS):
            s = dot(q_v[rows, cols(h)], kmt[h])
            e = jnp.exp2((s - jnp.max(s, axis=1, keepdims=True)) * SCALE2)
            near[h, rows, :] = (e * (1.0 / jnp.sum(e, axis=1, keepdims=True))).astype(BF16)
        return 0

    lax.fori_loop(0, SEGS, near_softmax, 0)

    for copy in rs_total:
        copy.wait_recv()

    top = jnp.max(fact_recv[...], axis=0)

    def combine(s, carry):
        num, den = carry
        lines = fact_recv[s]
        e = jnp.exp2((lines - top) * SCALE2)
        w = jnp.concatenate([e[0:1], e[1:2]], axis=1)
        part = jnp.concatenate([lines[2:3], lines[3:4]], axis=1)
        return num + rs_recv[s].astype(F32) * w, den + part * w

    num, den = lax.fori_loop(
        0,
        SEQN,
        combine,
        (jnp.zeros((SLICE, LANDMARKS), F32), jnp.zeros((1, LANDMARKS), F32)),
        unroll=4,
    )
    reduced = (num / den).astype(BF16)
    slot = (h_me // 2) * OWN + j_me
    rd_all[slot] = reduced
    for r in range(1, CHIPS):
        group_copy(rd_all, (slot,), (mp_s, mp_r), 0, across(r)).start()
    rd_total = group_copy(rd_all, (pl.ds(0, CHIPS - 1),), (mp_s, mp_r), 0, other)
    mp_out = group_copy(mp_all, (cme,), (mp_s, mp_r), 1, other)
    mp_in = group_copy(mp_all, (1 - cme,), (mp_s, mp_r), 1, other)

    for n in range(2):
        m = mid[cme + 2 * n]
        x_ref[n, 0:LANDMARKS, :] = dot(m.T.astype(BF16), m.astype(BF16))
        x_ref[n, LANDMARKS:, :] = m
    top_total[0].wait_recv()

    best = jnp.max(tops[...], axis=0)
    scale = 1.0 / (best[0:1, 0:1] * best[4:5, 0:1])
    xs = [x_ref[n] * scale for n in range(2)]
    for sweep in range(SWEEPS):
        for n in range(2):
            x = xs[n]
            xb = x.astype(BF16)
            y = dot(xb, xb[:LANDMARKS])
            b = (7.0 * x[:LANDMARKS] - y[:LANDMARKS]).astype(BF16)
            if sweep == SWEEPS - 1:
                x, y = x[LANDMARKS:], y[LANDMARKS:]
            xs[n] = 0.25 * (13.0 * x - 15.0 * y + dot(y.astype(BF16), b))
    iterated = [x.astype(BF16) for x in xs]

    rd_total.wait_recv()

    for n in range(2):
        rows = rd_all[n * OWN : (n + 1) * OWN].reshape(HEAD_DIM, LANDMARKS)
        mp_all[cme, n] = dot(rows, iterated[n]).astype(BF16)
    mp_out.start()

    def attend(h):
        lanes = pl.ds(pl.multiple_of(h * HEAD_DIM, HEAD_DIM), HEAD_DIM)
        mapped = mp_all[h % 2, h // 2].astype(F32).T.astype(BF16)
        for i in range(4):
            rows = slice(i * 512, (i + 1) * 512)
            out[rows, lanes] = (dot(near[h, rows, :], mapped) + conv[rows, lanes]).astype(BF16)

    attend(cme)
    attend(cme + 2)

    mp_in.wait_recv()

    attend(1 - cme)
    attend(3 - cme)

    down.wait_send()
    up.wait_send()
    for copy in lm_total + lm_out:
        copy.wait_send()
    @pl.when(cme == 1)
    def _():
        for copy in top_total:
            copy.wait_send()

    for copy in rs_total:
        copy.wait_send()
    rd_total.wait_send()
    mp_out.wait_send()


def shards(q, k, v, qs, ks, vs, cw):
    dma = pltpu.SemaphoreType.DMA
    vm = pltpu.VMEM
    hbm = pl.BlockSpec(memory_space=pl.ANY)
    whole = pl.BlockSpec(memory_space=pltpu.VMEM)
    taps = jnp.pad(cw, ((0, 0), (0, TOK - TAPS)))
    small = jnp.concatenate([qs.T, ks.T, vs.T, taps], axis=0)
    return pl.pallas_call(
        kernel,
        out_shape=jax.ShapeDtypeStruct((TOK, WIDTH), BF16),
        in_specs=[hbm, hbm, hbm, whole],
        out_specs=whole,
        scratch_shapes=[
            vm((TOK, WIDTH), BF16),
            vm((TOK, WIDTH), BF16),
            vm((TOK, WIDTH), BF16),
            vm((TOK + 128, WIDTH), BF16),
            vm((HEADS, HEAD_DIM, TOK), BF16),
            vm((TOK, 8), F32),
            vm((TOK, 8), F32),
            vm((2, 2, CHIPS, 2 * SEGS, WIDTH // 2), BF16),
            vm((HEADS, LANDMARKS, HEAD_DIM), BF16),
            vm((HEADS, HEAD_DIM, LANDMARKS), BF16),
            vm((HEADS, LANDMARKS, LANDMARKS), F32),
            vm((HEADN, 8, 128), F32),
            vm((2, TOK, LANDMARKS), F32),
            vm((2, TOK, LANDMARKS), BF16),
            vm((SEQN, SLICE, LANDMARKS), BF16),
            vm((SEQN, SLICE, LANDMARKS), BF16),
            vm((SEQN, 4, 128), F32),
            vm((SEQN, 4, 128), F32),
            vm((2, 2 * LANDMARKS, LANDMARKS), F32),
            vm((HEADS, TOK, LANDMARKS), BF16),
            vm((TOK, WIDTH), F32),
            vm((CHIPS, SLICE, LANDMARKS), BF16),
            vm((2, 2, HEAD_DIM, LANDMARKS), BF16),
            vm((HEADS, 128, 256), BF16),
            dma((SEGS,)),
            dma((SEGS,)),
            dma((SEGS,)),
            dma((4,)),
            dma((4,)),
            dma((2,)),
            dma((2,)),
            dma((2,)),
            dma((2,)),
            dma((2,)),
            dma((2,)),
            dma((2,)),
            dma((2,)),
            pltpu.SemaphoreType.REGULAR,
        ],
        compiler_params=pltpu.CompilerParams(
            collective_id=0, has_side_effects=True, vmem_limit_bytes=50 * 1024 * 1024
        ),
        name="nystrom",
    )(q, k, v, small)


def solution(mesh):
    tokens, heads = P("seq", "head"), P("head", None)
    return jax.shard_map(
        shards, mesh=mesh, in_specs=(tokens,) * 6 + (heads,), out_specs=tokens, check_vma=False
    )
```

```python
import functools
import math

import jax
import jax.numpy as jnp
from jax import lax
from jax.experimental import pallas as pl
from jax.experimental.pallas import tpu as pltpu
from jax.sharding import PartitionSpec as P

MESH = pl.DeviceIdType.MESH
F32 = jnp.float32
BF16 = jnp.bfloat16
HEAD_DIM = 128
LANDMARKS = 256
SWEEPS = 6
TAPS = 33
REACH = TAPS // 2
LOG2E = math.log2(math.e)
SCALE2 = HEAD_DIM**-0.5 * LOG2E
FACTOR = HEAD_DIM**-0.5

TOK = 2048
HEADS = 4
WIDTH = HEADS * HEAD_DIM
SEQN = 32
HEADN = 8
SEGS = 8
SEG = 256
CHIPS = SEQN // 2
OWN = 8
SLICE = HEAD_DIM // OWN
KEYS_EARLY = 3


def dot(a, b):
    return jnp.dot(a, b, preferred_element_type=F32)


def dot_nt(a, b):
    return lax.dot_general(a, b, (((1,), (1,)), ((), ())), preferred_element_type=F32)


def cols(h):
    return slice(h * HEAD_DIM, (h + 1) * HEAD_DIM)


def kernel(
    q_hbm, k_hbm, v_hbm, small, out,
    q_v, k_v, v_raw, v_pad, vt, sc_qk, sc_v, lm_all, qm, kmt,
    mid, tops, score, wt, rs_send, rs_recv, fact_send, fact_recv, x_ref, near, conv, rd_all, mp_all, toep,
    q_sem, k_sem, v_sem, lm_s, lm_r, halo_s, halo_r, top_s, top_r, rs_s, rs_r, mp_s, mp_r, go_sem,
):
    me = lax.axis_index("seq")
    zme = lax.axis_index("head")
    yme, xme, cme = me // 8, (me // 2) % 4, me % 2
    h_me = 2 * ((xme + yme) % 2) + cme
    j_me = (me // 2) // 2
    chip = me // 2
    other = me + 1 - 2 * cme

    def partner(r):
        return (
            ((yme + r // 8) % 4) * 8 + ((xme + (r // 2) % 4) % 4) * 2 + (cme + r % 2) % 2
        )

    def across(r):
        return ((yme + r // 4) % 4) * 8 + ((xme + r % 4) % 4) * 2 + cme

    def owner(h, j):
        y = j // 2
        return (4 * y + 2 * (j % 2) + (h // 2 + y) % 2) * 2 + h % 2

    def rows_copy(src, dst, sem, i):
        rows = pl.ds(i * SEG, SEG)
        return pltpu.make_async_copy(src.at[rows], dst.at[rows], sem.at[i])

    for i in range(SEGS):
        rows_copy(q_hbm, q_v, q_sem, i).start()
    for i in range(SEGS):
        rows_copy(k_hbm, k_v, k_sem, i).start()
    for i in range(SEGS):
        rows_copy(v_hbm, v_raw, v_sem, i).start()

    barrier = pltpu.get_barrier_semaphore()

    for r in range(1, CHIPS):
        target = ((yme + r // 4) % 4) * 8 + ((xme + r % 4) % 4) * 2
        pl.semaphore_signal(barrier, inc=1, device_id=(target, zme), device_id_type=MESH)

    @pl.when(cme == 1)
    def _():
        pl.semaphore_signal(barrier, inc=1, device_id=(other, zme), device_id_type=MESH)

    sc_qk[...] = small[0 : 2 * HEADS, :].T

    seg_id = lax.broadcasted_iota(jnp.int32, (SEGS, HEAD_DIM), 0)

    no_marks = (jnp.zeros((SEGS, HEAD_DIM), F32),) * HEADS

    def scale_means(t, src, buf, sem, first, end, marks):
        def segment(i, marks):
            rows = pl.ds(pl.multiple_of(i * SEG, SEG), SEG)
            rows_copy(src, buf, sem, i).wait()
            following = []
            for h in range(HEADS):
                n = t * HEADS + h
                x = (buf[rows, cols(h)].astype(F32) * sc_qk[rows, n : n + 1]).astype(BF16)
                buf[rows, cols(h)] = x
                mean = jnp.sum(x.astype(F32), axis=0, keepdims=True) * (1.0 / SEG)
                following.append(jnp.where(seg_id == i, mean, marks[h]))
            return tuple(following)

        return lax.fori_loop(first, end, segment, marks)

    def own_marks(t, marks):
        for n in range(2):
            both = jnp.concatenate([marks[n], marks[n + 2]], axis=0)
            lm_all[t, cme, chip, :, cols(n)] = both.astype(BF16)

    own_marks(0, scale_means(0, q_hbm, q_v, q_sem, 0, SEGS, no_marks))
    key_marks = scale_means(1, k_hbm, k_v, k_sem, 0, KEYS_EARLY, no_marks)

    @pl.when(cme == 0)
    def _():
        pl.semaphore_wait(barrier, SEQN - 1)
        pl.semaphore_signal(go_sem, inc=1, device_id=(other, zme), device_id_type=MESH)

    @pl.when(cme == 1)
    def _():
        pl.semaphore_wait(go_sem, 1)
        for r in range(1, HEADN):
            pl.semaphore_signal(
                barrier, inc=1, device_id=(me, (zme + r) % HEADN), device_id_type=MESH
            )

    def group_copy(buf, at, sems, n, target):
        return pltpu.make_async_remote_copy(
            src_ref=buf.at[at],
            dst_ref=buf.at[at],
            send_sem=sems[0].at[n],
            recv_sem=sems[1].at[n],
            device_id=(target, zme),
            device_id_type=MESH,
        )

    def leave(t):
        for r in range(1, CHIPS):
            group_copy(lm_all, (t, cme, chip), (lm_s, lm_r), t, across(r)).start()

    lm_total = [
        group_copy(lm_all, (t, 0, pl.ds(0, CHIPS - 1)), (lm_s, lm_r), t, other) for t in range(2)
    ]
    lm_out = [group_copy(lm_all, (t, cme), (lm_s, lm_r), 2 + t, other) for t in range(2)]
    lm_in = [group_copy(lm_all, (t, 1 - cme), (lm_s, lm_r), 2 + t, other) for t in range(2)]
    leave(0)

    own_marks(1, scale_means(1, k_hbm, k_v, k_sem, KEYS_EARLY, SEGS, key_marks))
    leave(1)

    sc_v[...] = small[2 * HEADS : 4 * HEADS, :].T
    def scale_v(i, _):
        rows = pl.ds(pl.multiple_of(i * SEG, SEG), SEG)
        out_rows = pl.ds(pl.multiple_of(i * SEG + REACH, REACH), SEG)
        rows_copy(v_hbm, v_raw, v_sem, i).wait()
        for h in range(HEADS):
            x = (v_raw[rows, cols(h)].astype(F32) * sc_v[rows, h : h + 1]).astype(BF16)
            v_pad[out_rows, cols(h)] = x
            vt[h, :, rows] = x.astype(F32).T.astype(BF16)
        return 0

    lax.fori_loop(0, SEGS, scale_v, 0, unroll=2)
    v_pad[TOK + 2 * REACH :, :] = jnp.zeros((128 - 2 * REACH, WIDTH), BF16)

    after, before = (me + 1) % SEQN, (me + SEQN - 1) % SEQN
    down = pltpu.make_async_remote_copy(
        src_ref=v_pad.at[pl.ds(TOK, REACH)],
        dst_ref=v_pad.at[pl.ds(0, REACH)],
        send_sem=halo_s.at[0],
        recv_sem=halo_r.at[0],
        device_id=(after, zme),
        device_id_type=MESH,
    )
    up = pltpu.make_async_remote_copy(
        src_ref=v_pad.at[pl.ds(REACH, REACH)],
        dst_ref=v_pad.at[pl.ds(TOK + REACH, REACH)],
        send_sem=halo_s.at[1],
        recv_sem=halo_r.at[1],
        device_id=(before, zme),
        device_id_type=MESH,
    )
    down.start()
    up.start()

    for h in range(HEADS):
        line = jnp.broadcast_to(small[3 * HEADS + h : 3 * HEADS + h + 1, 0:256], (128, 256))
        toep[h] = pltpu.roll(line, 0, 1, stride=1, stride_axis=0).astype(BF16)

    def conv_block(b):
        window = pl.ds(pl.multiple_of(b * 128, 128), 256)
        rows = pl.ds(pl.multiple_of(b * 128, 128), 128)
        for h in range(HEADS):
            conv[rows, cols(h)] = dot(toep[h], v_pad[window, cols(h)])

    def conv_inner(b, _):
        conv_block(b)
        return 0

    lm_total[0].wait_recv()
    lm_out[0].start()

    lax.fori_loop(1, TOK // 128 - 1, conv_inner, 0, unroll=True)

    lm_total[1].wait_recv()
    lm_out[1].start()

    lm_in[0].wait_recv()

    def by_head(t, h):
        both = lm_all[t, :, :, :, cols(h % 2)].reshape(SEQN, 2 * SEGS, HEAD_DIM).astype(F32)
        at = (h // 2) * SEGS
        return both[:, at : at + SEGS].reshape(LANDMARKS, HEAD_DIM)

    for h in range(HEADS):
        qm[h] = by_head(0, h).astype(BF16)

    def rs_copy(bufs, n, block, slot, target):
        return pltpu.make_async_remote_copy(
            src_ref=bufs[0].at[block],
            dst_ref=bufs[1].at[slot],
            send_sem=rs_s.at[n],
            recv_sem=rs_r.at[n],
            device_id=(target, zme),
            device_id_type=MESH,
        )

    sums, facts = (rs_send, rs_recv), (fact_send, fact_recv)
    tops_of, totals_of = {}, {}

    def far_scores(h):
        def chunk(i, top):
            rows = pl.ds(pl.multiple_of(i * SEG, SEG), SEG)
            s = dot_nt(k_v[rows, cols(h)], qm[h])
            score[h % 2, rows, :] = s
            return jnp.maximum(top, jnp.max(s.reshape(SEG // 8, 8, LANDMARKS), axis=0))

        top = lax.fori_loop(
            0, SEGS, chunk, jnp.full((8, LANDMARKS), -jnp.inf, F32), unroll=True
        )
        tops_of[h] = jnp.max(top, axis=0, keepdims=True)

    def far_weights(h):
        top = tops_of[h]

        def chunk(i, total):
            rows = pl.ds(pl.multiple_of(i * SEG, SEG), SEG)
            e = jnp.exp2((score[h % 2, rows, :] - top) * SCALE2)
            wt[h % 2, rows, :] = e.astype(BF16)
            return total + jnp.sum(e.reshape(SEG // 8, 8, LANDMARKS), axis=0)

        total = lax.fori_loop(0, SEGS, chunk, jnp.zeros((8, LANDMARKS), F32), unroll=True)
        totals_of[h] = jnp.sum(total, axis=0, keepdims=True)

    def far_sums(h):
        total = totals_of[h]
        summed = dot(vt[h], wt[h % 2]) * (1.0 / total)
        rs_send[h * OWN : (h + 1) * OWN] = summed.astype(BF16).reshape(OWN, SLICE, LANDMARKS)
        level = tops_of[h] * SCALE2 + jnp.log(total) * LOG2E
        lines = jnp.concatenate([level[:, :128], level[:, 128:]], axis=0)
        fact_send[h * OWN : (h + 1) * OWN] = jnp.broadcast_to(lines[None], (OWN, 2, 128))

    def far_leave(h):
        for n in range(1, OWN):
            j = (n + j_me) % OWN
            target = owner(h, j)
            rs_copy(sums, 0, h * OWN + j, me, target).start()
            rs_copy(facts, 1, h * OWN + j, me, target).start()

    far_scores(0)
    far_scores(1)
    far_weights(0)
    far_sums(0)
    far_leave(0)

    lm_in[1].wait_recv()
    for h in range(HEADS):
        kmt[h] = by_head(1, h).T.astype(BF16)

    col_top = jnp.zeros((1, 1), F32)
    row_top = jnp.zeros((1, 1), F32)
    for h in range(HEADS):
        s = dot(qm[h], kmt[h])
        e = jnp.exp2((s - jnp.max(s, axis=1, keepdims=True)) * SCALE2)
        m = e / jnp.sum(e, axis=1, keepdims=True)
        mid[h] = m
        c = jnp.sum(m, axis=0, keepdims=True)
        r = jnp.sum(m, axis=1, keepdims=True)
        col_top = jnp.maximum(col_top, jnp.max(c, axis=1, keepdims=True))
        row_top = jnp.maximum(row_top, jnp.max(r, axis=0, keepdims=True))
    first_half = lax.broadcasted_iota(jnp.int32, (8, 128), 0) < 4
    own_top = jnp.where(
        first_half, jnp.broadcast_to(col_top, (8, 128)), jnp.broadcast_to(row_top, (8, 128))
    )

    tops[zme] = own_top

    def top_copy(at, core, target):
        return pltpu.make_async_remote_copy(
            src_ref=tops.at[at],
            dst_ref=tops.at[at],
            send_sem=top_s.at[core],
            recv_sem=top_r.at[0],
            device_id=(2 * chip + core, target),
            device_id_type=MESH,
        )

    @pl.when(cme == 1)
    def _():
        pl.semaphore_wait(barrier, HEADN - 1)
        for r in range(1, HEADN):
            top_copy(zme, 0, (zme + r) % HEADN).start()
            top_copy(zme, 1, (zme + r) % HEADN).start()

    top_total = [top_copy(pl.ds(0, HEADN - 1), core, zme) for core in range(2)]

    far_scores(2)
    far_weights(1)
    far_sums(1)
    far_scores(3)
    far_leave(1)
    far_weights(2)
    far_sums(2)
    far_weights(3)
    far_leave(2)
    far_sums(3)
    far_leave(3)
    for n in range(1, HEADS):
        h = (h_me + n) % HEADS
        rs_copy(sums, 0, h * OWN + j_me, me, owner(h, j_me)).start()
        rs_copy(facts, 1, h * OWN + j_me, me, owner(h, j_me)).start()
    rs_total = [
        rs_copy(bufs, n, pl.ds(0, SEQN - 1), pl.ds(0, SEQN - 1), other)
        for n, bufs in enumerate((sums, facts))
    ]
    rs_recv[me] = rs_send[h_me * OWN + j_me]
    fact_recv[me] = fact_send[h_me * OWN + j_me]

    down.wait_recv()
    up.wait_recv()
    v_pad[0:REACH, :] = jnp.where(me == 0, jnp.zeros((REACH, WIDTH), BF16), v_pad[0:REACH, :])
    v_pad[TOK + REACH : TOK + 2 * REACH, :] = jnp.where(
        me == SEQN - 1, jnp.zeros((REACH, WIDTH), BF16), v_pad[TOK + REACH : TOK + 2 * REACH, :]
    )
    conv_block(0)
    conv_block(TOK // 128 - 1)

    def near_softmax(i, _):
        rows = pl.ds(pl.multiple_of(i * SEG, SEG), SEG)
        for h in range(HEADS):
            s = dot(q_v[rows, cols(h)], kmt[h])
            e = jnp.exp2((s - jnp.max(s, axis=1, keepdims=True)) * SCALE2)
            near[h, rows, :] = (e * (1.0 / jnp.sum(e, axis=1, keepdims=True))).astype(BF16)
        return 0

    lax.fori_loop(0, SEGS, near_softmax, 0)

    for copy in rs_total:
        copy.wait_recv()

    top = jnp.max(fact_recv[...], axis=0)

    def combine(s, carry):
        num, den = carry
        e = jnp.exp2(fact_recv[s] - top)
        w = jnp.concatenate([e[0:1], e[1:2]], axis=1)
        return num + rs_recv[s].astype(F32) * w, den + w

    num, den = lax.fori_loop(
        0,
        SEQN,
        combine,
        (jnp.zeros((SLICE, LANDMARKS), F32), jnp.zeros((1, LANDMARKS), F32)),
        unroll=4,
    )
    reduced = (num / den).astype(BF16)
    slot = (h_me // 2) * OWN + j_me
    rd_all[slot] = reduced
    for r in range(1, CHIPS):
        group_copy(rd_all, (slot,), (mp_s, mp_r), 0, across(r)).start()
    rd_total = group_copy(rd_all, (pl.ds(0, CHIPS - 1),), (mp_s, mp_r), 0, other)
    mp_out = group_copy(mp_all, (cme,), (mp_s, mp_r), 1, other)
    mp_in = group_copy(mp_all, (1 - cme,), (mp_s, mp_r), 1, other)

    for n in range(2):
        m = mid[cme + 2 * n]
        x_ref[n, 0:LANDMARKS, :] = dot(m.T.astype(BF16), m.astype(BF16))
        x_ref[n, LANDMARKS:, :] = m
    top_total[0].wait_recv()

    best = jnp.max(tops[...], axis=0)
    scale = 1.0 / (best[0:1, 0:1] * best[4:5, 0:1])
    xs = [x_ref[n] * scale for n in range(2)]
    for sweep in range(SWEEPS):
        for n in range(2):
            x = xs[n]
            xb = x.astype(BF16)
            y = dot(xb, xb[:LANDMARKS])
            b = (7.0 * x[:LANDMARKS] - y[:LANDMARKS]).astype(BF16)
            if sweep == SWEEPS - 1:
                x, y = x[LANDMARKS:], y[LANDMARKS:]
            xs[n] = 0.25 * (13.0 * x - 15.0 * y + dot(y.astype(BF16), b))
    iterated = [x.astype(BF16) for x in xs]

    rd_total.wait_recv()

    for n in range(2):
        rows = rd_all[n * OWN : (n + 1) * OWN].reshape(HEAD_DIM, LANDMARKS)
        mp_all[cme, n] = dot(rows, iterated[n]).astype(BF16)
    mp_out.start()

    def attend(h):
        lanes = pl.ds(pl.multiple_of(h * HEAD_DIM, HEAD_DIM), HEAD_DIM)
        mapped = mp_all[h % 2, h // 2].astype(F32).T.astype(BF16)
        for i in range(4):
            rows = slice(i * 512, (i + 1) * 512)
            out[rows, lanes] = (dot(near[h, rows, :], mapped) + conv[rows, lanes]).astype(BF16)

    attend(cme)
    attend(cme + 2)

    mp_in.wait_recv()

    attend(1 - cme)
    attend(3 - cme)

    down.wait_send()
    up.wait_send()
    for copy in lm_total + lm_out:
        copy.wait_send()
    @pl.when(cme == 1)
    def _():
        for copy in top_total:
            copy.wait_send()

    for copy in rs_total:
        copy.wait_send()
    rd_total.wait_send()
    mp_out.wait_send()


def shards(q, k, v, qs, ks, vs, cw):
    dma = pltpu.SemaphoreType.DMA
    vm = pltpu.VMEM
    hbm = pl.BlockSpec(memory_space=pl.ANY)
    whole = pl.BlockSpec(memory_space=pltpu.VMEM)
    taps = jnp.pad(cw, ((0, 0), (0, TOK - TAPS)))
    small = jnp.concatenate([qs.T, ks.T, vs.T, taps], axis=0)
    return pl.pallas_call(
        kernel,
        out_shape=jax.ShapeDtypeStruct((TOK, WIDTH), BF16),
        in_specs=[hbm, hbm, hbm, whole],
        out_specs=whole,
        scratch_shapes=[
            vm((TOK, WIDTH), BF16),
            vm((TOK, WIDTH), BF16),
            vm((TOK, WIDTH), BF16),
            vm((TOK + 128, WIDTH), BF16),
            vm((HEADS, HEAD_DIM, TOK), BF16),
            vm((TOK, 8), F32),
            vm((TOK, 8), F32),
            vm((2, 2, CHIPS, 2 * SEGS, WIDTH // 2), BF16),
            vm((HEADS, LANDMARKS, HEAD_DIM), BF16),
            vm((HEADS, HEAD_DIM, LANDMARKS), BF16),
            vm((HEADS, LANDMARKS, LANDMARKS), F32),
            vm((HEADN, 8, 128), F32),
            vm((2, TOK, LANDMARKS), F32),
            vm((2, TOK, LANDMARKS), BF16),
            vm((SEQN, SLICE, LANDMARKS), BF16),
            vm((SEQN, SLICE, LANDMARKS), BF16),
            vm((SEQN, 2, 128), F32),
            vm((SEQN, 2, 128), F32),
            vm((2, 2 * LANDMARKS, LANDMARKS), F32),
            vm((HEADS, TOK, LANDMARKS), BF16),
            vm((TOK, WIDTH), F32),
            vm((CHIPS, SLICE, LANDMARKS), BF16),
            vm((2, 2, HEAD_DIM, LANDMARKS), BF16),
            vm((HEADS, 128, 256), BF16),
            dma((SEGS,)),
            dma((SEGS,)),
            dma((SEGS,)),
            dma((4,)),
            dma((4,)),
            dma((2,)),
            dma((2,)),
            dma((2,)),
            dma((2,)),
            dma((2,)),
            dma((2,)),
            dma((2,)),
            dma((2,)),
            pltpu.SemaphoreType.REGULAR,
        ],
        compiler_params=pltpu.CompilerParams(
            collective_id=0, has_side_effects=True, vmem_limit_bytes=50 * 1024 * 1024
        ),
        name="nystrom",
    )(q, k, v, small)


def solution(mesh):
    tokens, heads = P("seq", "head"), P("head", None)
    return jax.shard_map(
        shards, mesh=mesh, in_specs=(tokens,) * 6 + (heads,), out_specs=tokens, check_vma=False
    )
```

```python
import functools
import math

import jax
import jax.numpy as jnp
from jax import lax
from jax.experimental import pallas as pl
from jax.experimental.pallas import tpu as pltpu
from jax.sharding import PartitionSpec as P

MESH = pl.DeviceIdType.MESH
F32 = jnp.float32
BF16 = jnp.bfloat16
HEAD_DIM = 128
LANDMARKS = 256
SWEEPS = 6
TAPS = 33
REACH = TAPS // 2
LOG2E = math.log2(math.e)
SCALE2 = HEAD_DIM**-0.5 * LOG2E
FACTOR = HEAD_DIM**-0.5

TOK = 2048
HEADS = 4
WIDTH = HEADS * HEAD_DIM
SEQN = 32
HEADN = 8
SEGS = 8
SEG = 256
CHIPS = SEQN // 2
OWN = 8
SLICE = HEAD_DIM // OWN
KEYS_EARLY = 3


def hops(r):
    return min(r // 4, 4 - r // 4) + min(r % 4, 4 - r % 4)


FAR_FIRST = sorted(range(1, CHIPS), key=hops, reverse=True)


def dot(a, b):
    return jnp.dot(a, b, preferred_element_type=F32)


def dot_nt(a, b):
    return lax.dot_general(a, b, (((1,), (1,)), ((), ())), preferred_element_type=F32)


def cols(h):
    return slice(h * HEAD_DIM, (h + 1) * HEAD_DIM)


def kernel(
    q_hbm, k_hbm, v_hbm, small, out,
    q_v, k_v, v_raw, v_pad, vt, sc_qk, sc_v, lm_all, qm, kmt,
    mid, tops, score, wt, rs_send, rs_recv, fact_send, fact_recv, x_ref, near, conv, rd_all, mp_all, toep,
    q_sem, k_sem, v_sem, lm_s, lm_r, halo_s, halo_r, top_s, top_r, rs_s, rs_r, mp_s, mp_r, go_sem,
):
    me = lax.axis_index("seq")
    zme = lax.axis_index("head")
    yme, xme, cme = me // 8, (me // 2) % 4, me % 2
    h_me = 2 * ((xme + yme) % 2) + cme
    j_me = (me // 2) // 2
    chip = me // 2
    other = me + 1 - 2 * cme

    def partner(r):
        return (
            ((yme + r // 8) % 4) * 8 + ((xme + (r // 2) % 4) % 4) * 2 + (cme + r % 2) % 2
        )

    def across(r):
        return ((yme + r // 4) % 4) * 8 + ((xme + r % 4) % 4) * 2 + cme

    def owner(h, j):
        y = j // 2
        return (4 * y + 2 * (j % 2) + (h // 2 + y) % 2) * 2 + h % 2

    def rows_copy(src, dst, sem, i):
        rows = pl.ds(i * SEG, SEG)
        return pltpu.make_async_copy(src.at[rows], dst.at[rows], sem.at[i])

    for i in range(SEGS):
        rows_copy(q_hbm, q_v, q_sem, i).start()
    for i in range(SEGS):
        rows_copy(k_hbm, k_v, k_sem, i).start()
    for i in range(SEGS):
        rows_copy(v_hbm, v_raw, v_sem, i).start()

    barrier = pltpu.get_barrier_semaphore()

    for r in FAR_FIRST:
        target = ((yme + r // 4) % 4) * 8 + ((xme + r % 4) % 4) * 2
        pl.semaphore_signal(barrier, inc=1, device_id=(target, zme), device_id_type=MESH)

    @pl.when(cme == 1)
    def _():
        pl.semaphore_signal(barrier, inc=1, device_id=(other, zme), device_id_type=MESH)

    sc_qk[...] = small[0 : 2 * HEADS, :].T

    seg_id = lax.broadcasted_iota(jnp.int32, (SEGS, HEAD_DIM), 0)

    no_marks = (jnp.zeros((SEGS, HEAD_DIM), F32),) * HEADS

    def scale_means(t, src, buf, sem, first, end, marks):
        def segment(i, marks):
            rows = pl.ds(pl.multiple_of(i * SEG, SEG), SEG)
            rows_copy(src, buf, sem, i).wait()
            following = []
            for h in range(HEADS):
                n = t * HEADS + h
                x = (buf[rows, cols(h)].astype(F32) * sc_qk[rows, n : n + 1]).astype(BF16)
                buf[rows, cols(h)] = x
                mean = jnp.sum(x.astype(F32), axis=0, keepdims=True) * (1.0 / SEG)
                following.append(jnp.where(seg_id == i, mean, marks[h]))
            return tuple(following)

        return lax.fori_loop(first, end, segment, marks)

    def own_marks(t, marks):
        for n in range(2):
            both = jnp.concatenate([marks[n], marks[n + 2]], axis=0)
            lm_all[t, cme, chip, :, cols(n)] = both.astype(BF16)

    own_marks(0, scale_means(0, q_hbm, q_v, q_sem, 0, SEGS, no_marks))
    key_marks = scale_means(1, k_hbm, k_v, k_sem, 0, KEYS_EARLY, no_marks)

    @pl.when(cme == 0)
    def _():
        pl.semaphore_wait(barrier, SEQN - 1)
        pl.semaphore_signal(go_sem, inc=1, device_id=(other, zme), device_id_type=MESH)

    @pl.when(cme == 1)
    def _():
        pl.semaphore_wait(go_sem, 1)
        for r in range(1, HEADN):
            pl.semaphore_signal(
                barrier, inc=1, device_id=(me, (zme + r) % HEADN), device_id_type=MESH
            )

    def group_copy(buf, at, sems, n, target):
        return pltpu.make_async_remote_copy(
            src_ref=buf.at[at],
            dst_ref=buf.at[at],
            send_sem=sems[0].at[n],
            recv_sem=sems[1].at[n],
            device_id=(target, zme),
            device_id_type=MESH,
        )

    def leave(t):
        for r in FAR_FIRST:
            group_copy(lm_all, (t, cme, chip), (lm_s, lm_r), t, across(r)).start()

    lm_total = [
        group_copy(lm_all, (t, 0, pl.ds(0, CHIPS - 1)), (lm_s, lm_r), t, other) for t in range(2)
    ]
    lm_out = [group_copy(lm_all, (t, cme), (lm_s, lm_r), 2 + t, other) for t in range(2)]
    lm_in = [group_copy(lm_all, (t, 1 - cme), (lm_s, lm_r), 2 + t, other) for t in range(2)]
    leave(0)

    own_marks(1, scale_means(1, k_hbm, k_v, k_sem, KEYS_EARLY, SEGS, key_marks))
    leave(1)

    sc_v[...] = small[2 * HEADS : 4 * HEADS, :].T
    def scale_v(i, _):
        rows = pl.ds(pl.multiple_of(i * SEG, SEG), SEG)
        out_rows = pl.ds(pl.multiple_of(i * SEG + REACH, REACH), SEG)
        rows_copy(v_hbm, v_raw, v_sem, i).wait()
        for h in range(HEADS):
            x = (v_raw[rows, cols(h)].astype(F32) * sc_v[rows, h : h + 1]).astype(BF16)
            v_pad[out_rows, cols(h)] = x
            vt[h, :, rows] = x.astype(F32).T.astype(BF16)
        return 0

    lax.fori_loop(0, SEGS, scale_v, 0, unroll=2)
    v_pad[TOK + 2 * REACH :, :] = jnp.zeros((128 - 2 * REACH, WIDTH), BF16)

    after, before = (me + 1) % SEQN, (me + SEQN - 1) % SEQN
    down = pltpu.make_async_remote_copy(
        src_ref=v_pad.at[pl.ds(TOK, REACH)],
        dst_ref=v_pad.at[pl.ds(0, REACH)],
        send_sem=halo_s.at[0],
        recv_sem=halo_r.at[0],
        device_id=(after, zme),
        device_id_type=MESH,
    )
    up = pltpu.make_async_remote_copy(
        src_ref=v_pad.at[pl.ds(REACH, REACH)],
        dst_ref=v_pad.at[pl.ds(TOK + REACH, REACH)],
        send_sem=halo_s.at[1],
        recv_sem=halo_r.at[1],
        device_id=(before, zme),
        device_id_type=MESH,
    )
    down.start()
    up.start()

    for h in range(HEADS):
        line = jnp.broadcast_to(small[3 * HEADS + h : 3 * HEADS + h + 1, 0:256], (128, 256))
        toep[h] = pltpu.roll(line, 0, 1, stride=1, stride_axis=0).astype(BF16)

    def conv_block(b):
        window = pl.ds(pl.multiple_of(b * 128, 128), 256)
        rows = pl.ds(pl.multiple_of(b * 128, 128), 128)
        for h in range(HEADS):
            conv[rows, cols(h)] = dot(toep[h], v_pad[window, cols(h)])

    def conv_inner(b, _):
        conv_block(b)
        return 0

    lm_total[0].wait_recv()
    lm_out[0].start()

    lax.fori_loop(1, TOK // 128 - 1, conv_inner, 0, unroll=True)

    lm_total[1].wait_recv()
    lm_out[1].start()

    lm_in[0].wait_recv()

    def by_head(t, h):
        both = lm_all[t, :, :, :, cols(h % 2)].reshape(SEQN, 2 * SEGS, HEAD_DIM).astype(F32)
        at = (h // 2) * SEGS
        return both[:, at : at + SEGS].reshape(LANDMARKS, HEAD_DIM)

    for h in range(HEADS):
        qm[h] = by_head(0, h).astype(BF16)

    def rs_copy(bufs, n, block, slot, target):
        return pltpu.make_async_remote_copy(
            src_ref=bufs[0].at[block],
            dst_ref=bufs[1].at[slot],
            send_sem=rs_s.at[n],
            recv_sem=rs_r.at[n],
            device_id=(target, zme),
            device_id_type=MESH,
        )

    sums, facts = (rs_send, rs_recv), (fact_send, fact_recv)
    tops_of, totals_of = {}, {}

    def far_scores(h):
        def chunk(i, top):
            rows = pl.ds(pl.multiple_of(i * SEG, SEG), SEG)
            s = dot_nt(k_v[rows, cols(h)], qm[h])
            score[h % 2, rows, :] = s
            return jnp.maximum(top, jnp.max(s.reshape(SEG // 8, 8, LANDMARKS), axis=0))

        top = lax.fori_loop(
            0, SEGS, chunk, jnp.full((8, LANDMARKS), -jnp.inf, F32), unroll=True
        )
        tops_of[h] = jnp.max(top, axis=0, keepdims=True)

    def far_weights(h):
        top = tops_of[h]

        def chunk(i, total):
            rows = pl.ds(pl.multiple_of(i * SEG, SEG), SEG)
            e = jnp.exp2((score[h % 2, rows, :] - top) * SCALE2)
            wt[h % 2, rows, :] = e.astype(BF16)
            return total + jnp.sum(e.reshape(SEG // 8, 8, LANDMARKS), axis=0)

        total = lax.fori_loop(0, SEGS, chunk, jnp.zeros((8, LANDMARKS), F32), unroll=True)
        totals_of[h] = jnp.sum(total, axis=0, keepdims=True)

    def far_sums(h):
        total = totals_of[h]
        summed = dot(vt[h], wt[h % 2]) * (1.0 / total)
        rs_send[h * OWN : (h + 1) * OWN] = summed.astype(BF16).reshape(OWN, SLICE, LANDMARKS)
        level = tops_of[h] * SCALE2 + jnp.log(total) * LOG2E
        lines = jnp.concatenate([level[:, :128], level[:, 128:]], axis=0)
        fact_send[h * OWN : (h + 1) * OWN] = jnp.broadcast_to(lines[None], (OWN, 2, 128))

    def far_leave(h):
        for n in range(1, OWN):
            j = (n + j_me) % OWN
            target = owner(h, j)
            rs_copy(sums, 0, h * OWN + j, me, target).start()
            rs_copy(facts, 1, h * OWN + j, me, target).start()

    far_scores(0)
    far_scores(1)
    far_weights(0)
    far_sums(0)
    far_leave(0)

    lm_in[1].wait_recv()
    for h in range(HEADS):
        kmt[h] = by_head(1, h).T.astype(BF16)

    col_top = jnp.zeros((1, 1), F32)
    row_top = jnp.zeros((1, 1), F32)
    for h in range(HEADS):
        s = dot(qm[h], kmt[h])
        e = jnp.exp2((s - jnp.max(s, axis=1, keepdims=True)) * SCALE2)
        m = e / jnp.sum(e, axis=1, keepdims=True)
        mid[h] = m
        c = jnp.sum(m, axis=0, keepdims=True)
        r = jnp.sum(m, axis=1, keepdims=True)
        col_top = jnp.maximum(col_top, jnp.max(c, axis=1, keepdims=True))
        row_top = jnp.maximum(row_top, jnp.max(r, axis=0, keepdims=True))
    first_half = lax.broadcasted_iota(jnp.int32, (8, 128), 0) < 4
    own_top = jnp.where(
        first_half, jnp.broadcast_to(col_top, (8, 128)), jnp.broadcast_to(row_top, (8, 128))
    )

    tops[zme] = own_top

    def top_copy(at, core, target):
        return pltpu.make_async_remote_copy(
            src_ref=tops.at[at],
            dst_ref=tops.at[at],
            send_sem=top_s.at[core],
            recv_sem=top_r.at[0],
            device_id=(2 * chip + core, target),
            device_id_type=MESH,
        )

    @pl.when(cme == 1)
    def _():
        pl.semaphore_wait(barrier, HEADN - 1)
        for r in range(1, HEADN):
            top_copy(zme, 0, (zme + r) % HEADN).start()
            top_copy(zme, 1, (zme + r) % HEADN).start()

    top_total = [top_copy(pl.ds(0, HEADN - 1), core, zme) for core in range(2)]

    far_scores(2)
    far_weights(1)
    far_sums(1)
    far_scores(3)
    far_leave(1)
    far_weights(2)
    far_sums(2)
    far_weights(3)
    far_leave(2)
    far_sums(3)
    far_leave(3)
    for n in range(1, HEADS):
        h = (h_me + n) % HEADS
        rs_copy(sums, 0, h * OWN + j_me, me, owner(h, j_me)).start()
        rs_copy(facts, 1, h * OWN + j_me, me, owner(h, j_me)).start()
    rs_total = [
        rs_copy(bufs, n, pl.ds(0, SEQN - 1), pl.ds(0, SEQN - 1), other)
        for n, bufs in enumerate((sums, facts))
    ]
    rs_recv[me] = rs_send[h_me * OWN + j_me]
    fact_recv[me] = fact_send[h_me * OWN + j_me]

    down.wait_recv()
    up.wait_recv()
    v_pad[0:REACH, :] = jnp.where(me == 0, jnp.zeros((REACH, WIDTH), BF16), v_pad[0:REACH, :])
    v_pad[TOK + REACH : TOK + 2 * REACH, :] = jnp.where(
        me == SEQN - 1, jnp.zeros((REACH, WIDTH), BF16), v_pad[TOK + REACH : TOK + 2 * REACH, :]
    )
    conv_block(0)
    conv_block(TOK // 128 - 1)

    def near_softmax(i, _):
        rows = pl.ds(pl.multiple_of(i * SEG, SEG), SEG)
        for h in range(HEADS):
            s = dot(q_v[rows, cols(h)], kmt[h])
            e = jnp.exp2((s - jnp.max(s, axis=1, keepdims=True)) * SCALE2)
            near[h, rows, :] = (e * (1.0 / jnp.sum(e, axis=1, keepdims=True))).astype(BF16)
        return 0

    lax.fori_loop(0, SEGS, near_softmax, 0)

    for copy in rs_total:
        copy.wait_recv()

    top = jnp.max(fact_recv[...], axis=0)

    def combine(s, carry):
        num, den = carry
        e = jnp.exp2(fact_recv[s] - top)
        w = jnp.concatenate([e[0:1], e[1:2]], axis=1)
        return num + rs_recv[s].astype(F32) * w, den + w

    num, den = lax.fori_loop(
        0,
        SEQN,
        combine,
        (jnp.zeros((SLICE, LANDMARKS), F32), jnp.zeros((1, LANDMARKS), F32)),
        unroll=4,
    )
    reduced = (num / den).astype(BF16)
    slot = (h_me // 2) * OWN + j_me
    rd_all[slot] = reduced
    for r in FAR_FIRST:
        group_copy(rd_all, (slot,), (mp_s, mp_r), 0, across(r)).start()
    rd_total = group_copy(rd_all, (pl.ds(0, CHIPS - 1),), (mp_s, mp_r), 0, other)
    mp_out = group_copy(mp_all, (cme,), (mp_s, mp_r), 1, other)
    mp_in = group_copy(mp_all, (1 - cme,), (mp_s, mp_r), 1, other)

    for n in range(2):
        m = mid[cme + 2 * n]
        x_ref[n, 0:LANDMARKS, :] = dot(m.T.astype(BF16), m.astype(BF16))
        x_ref[n, LANDMARKS:, :] = m
    top_total[0].wait_recv()

    best = jnp.max(tops[...], axis=0)
    scale = 1.0 / (best[0:1, 0:1] * best[4:5, 0:1])
    xs = [x_ref[n] * scale for n in range(2)]
    for sweep in range(SWEEPS):
        for n in range(2):
            x = xs[n]
            xb = x.astype(BF16)
            y = dot(xb, xb[:LANDMARKS])
            b = (7.0 * x[:LANDMARKS] - y[:LANDMARKS]).astype(BF16)
            if sweep == SWEEPS - 1:
                x, y = x[LANDMARKS:], y[LANDMARKS:]
            xs[n] = 0.25 * (13.0 * x - 15.0 * y + dot(y.astype(BF16), b))
    iterated = [x.astype(BF16) for x in xs]

    rd_total.wait_recv()

    for n in range(2):
        rows = rd_all[n * OWN : (n + 1) * OWN].reshape(HEAD_DIM, LANDMARKS)
        mp_all[cme, n] = dot(rows, iterated[n]).astype(BF16)
    mp_out.start()

    def attend(h):
        lanes = pl.ds(pl.multiple_of(h * HEAD_DIM, HEAD_DIM), HEAD_DIM)
        mapped = mp_all[h % 2, h // 2].astype(F32).T.astype(BF16)
        for i in range(4):
            rows = slice(i * 512, (i + 1) * 512)
            out[rows, lanes] = (dot(near[h, rows, :], mapped) + conv[rows, lanes]).astype(BF16)

    attend(cme)
    attend(cme + 2)

    mp_in.wait_recv()

    attend(1 - cme)
    attend(3 - cme)

    down.wait_send()
    up.wait_send()
    for copy in lm_total + lm_out:
        copy.wait_send()
    @pl.when(cme == 1)
    def _():
        for copy in top_total:
            copy.wait_send()

    for copy in rs_total:
        copy.wait_send()
    rd_total.wait_send()
    mp_out.wait_send()


def shards(q, k, v, qs, ks, vs, cw):
    dma = pltpu.SemaphoreType.DMA
    vm = pltpu.VMEM
    hbm = pl.BlockSpec(memory_space=pl.ANY)
    whole = pl.BlockSpec(memory_space=pltpu.VMEM)
    taps = jnp.pad(cw, ((0, 0), (0, TOK - TAPS)))
    small = jnp.concatenate([qs.T, ks.T, vs.T, taps], axis=0)
    return pl.pallas_call(
        kernel,
        out_shape=jax.ShapeDtypeStruct((TOK, WIDTH), BF16),
        in_specs=[hbm, hbm, hbm, whole],
        out_specs=whole,
        scratch_shapes=[
            vm((TOK, WIDTH), BF16),
            vm((TOK, WIDTH), BF16),
            vm((TOK, WIDTH), BF16),
            vm((TOK + 128, WIDTH), BF16),
            vm((HEADS, HEAD_DIM, TOK), BF16),
            vm((TOK, 8), F32),
            vm((TOK, 8), F32),
            vm((2, 2, CHIPS, 2 * SEGS, WIDTH // 2), BF16),
            vm((HEADS, LANDMARKS, HEAD_DIM), BF16),
            vm((HEADS, HEAD_DIM, LANDMARKS), BF16),
            vm((HEADS, LANDMARKS, LANDMARKS), F32),
            vm((HEADN, 8, 128), F32),
            vm((2, TOK, LANDMARKS), F32),
            vm((2, TOK, LANDMARKS), BF16),
            vm((SEQN, SLICE, LANDMARKS), BF16),
            vm((SEQN, SLICE, LANDMARKS), BF16),
            vm((SEQN, 2, 128), F32),
            vm((SEQN, 2, 128), F32),
            vm((2, 2 * LANDMARKS, LANDMARKS), F32),
            vm((HEADS, TOK, LANDMARKS), BF16),
            vm((TOK, WIDTH), F32),
            vm((CHIPS, SLICE, LANDMARKS), BF16),
            vm((2, 2, HEAD_DIM, LANDMARKS), BF16),
            vm((HEADS, 128, 256), BF16),
            dma((SEGS,)),
            dma((SEGS,)),
            dma((SEGS,)),
            dma((4,)),
            dma((4,)),
            dma((2,)),
            dma((2,)),
            dma((2,)),
            dma((2,)),
            dma((2,)),
            dma((2,)),
            dma((2,)),
            dma((2,)),
            pltpu.SemaphoreType.REGULAR,
        ],
        compiler_params=pltpu.CompilerParams(
            collective_id=0, has_side_effects=True, vmem_limit_bytes=50 * 1024 * 1024
        ),
        name="nystrom",
    )(q, k, v, small)


def solution(mesh):
    tokens, heads = P("seq", "head"), P("head", None)
    return jax.shard_map(
        shards, mesh=mesh, in_specs=(tokens,) * 6 + (heads,), out_specs=tokens, check_vma=False
    )
```
